512 devices in a mesh: blk: 128 (over z, y, core), ga: 4 (over x).
Axes of the slice: x: 4, y: 8, z: 8, core: 2. Of those that a mesh axis runs over, the one named last changes fastest.
Arguments:
- thermal_deviation: bfloat16 [32768, 128], P('blk', 'ga'), may hold values from -4 to 4
- moisture_mass: bfloat16 [32768, 128], P('blk', 'ga'), may hold values from 0.19921875 to 2
- condensate_optic: bfloat16 [32768, 128], P('blk', 'ga'), may hold values from 0.0099487305 to 1
- sun_height_factor: float32 [32768], P('blk'), may hold values from -1 to 1
- group_assignment: int32 [32768], P('blk'), may hold values from 0 to 127, as said below
- opacity_factor: float32 [256], P('ga'), may hold values from 0.001 to 0.03
- thermal_power: float32 [256], P('ga'), may hold values from -2 to 2
- sunlight_weights: float32 [256], P('ga'), may hold values from 0.2 to 2
- thermal_weights: float32 [256], P('ga'), may hold values from 0.05 to 0.5
Outputs:
- heating: float32 [32768, 128], P('blk', 'ga')
- surface: float32 [32768], P(('blk', 'ga'))
The draws below stay inside these ranges and needn't reach their ends.
Inputs may be any that keep to these rules, and one draw needn't show every extreme that they name: `group_assignment`: each dynamics block of 256 columns names every group exactly 2 times.
All inputs are finite; a program needn't handle non-finite values.
Results may differ from the reference program's by a relative error of at most 0.0013.
Values may be sent and summed in bfloat16 or wider, within the bound.
A program may use at most 64 MiB of HBM per device.

```python
import math
import jax
import jax.numpy as jnp
from jax import lax

L = 128
GPOINT_NUMBER = 256
COL_DEV = 256
COLS = 32768
N_BLK = 128


def draw_group_assignment(key, part):
    key = jax.random.fold_in(key, 11)
    base = jnp.tile(jnp.arange(N_BLK, dtype=jnp.int32), COL_DEV // N_BLK)
    keys = jax.random.split(key, N_BLK)
    rows = jax.vmap(lambda single: jax.random.permutation(single, base))(keys)
    return rows.reshape(-1).astype(jnp.int32)


def draw_thermal_deviation(key, part):
    key = jax.random.fold_in(key, 21)
    first_key = jax.random.fold_in(key, 0)
    values = jnp.clip(1.5 * jax.random.normal(first_key, (COLS, L), jnp.float32), -4.0, 4.0)
    return values.astype(jnp.bfloat16)


def draw_sun_height_factor(key, part):
    key = jax.random.fold_in(key, 31)
    values = jax.random.uniform(key, (COLS,), jnp.float32, -1.0, 1.0)
    return values.astype(jnp.float32)


def draw_sunlight_weights(key, part):
    key = jax.random.fold_in(key, 41)
    values = jnp.exp(jax.random.uniform(key, (GPOINT_NUMBER,), jnp.float32, jnp.log(0.2), jnp.log(2.0)))
    return jnp.clip(values, 0.2, 2.0).astype(jnp.float32)


def draw_thermal_weights(key, part):
    key = jax.random.fold_in(key, 51)
    values = jnp.exp(jax.random.uniform(key, (GPOINT_NUMBER,), jnp.float32, jnp.log(0.05), jnp.log(0.5)))
    return jnp.clip(values, 0.05, 0.5).astype(jnp.float32)


def block_levels(key, dims, pieces, smallest, high):
    factor_of = 1.0
    for axis_at, shards_of in pieces:
        draws = jax.random.uniform(jax.random.fold_in(jax.random.fold_in(key, 6), axis_at), (shards_of,), jnp.float32, smallest / len(pieces), high / len(pieces))
        factor_of = factor_of * jnp.repeat(jnp.exp(draws), dims[axis_at] // shards_of).reshape((-1,) + (1,) * (len(dims) - 1 - axis_at))
    return factor_of


def setup_inputs(seed: int = 0) -> dict:
    seeds = jax.random.split(jax.random.key(seed), 10)
    thermal_deviation = draw_thermal_deviation(jax.random.fold_in(seeds[9], 71), 0)
    moisture_mass = jnp.clip(jnp.exp(math.log(2.0) - 2.306499 * jax.random.uniform(seeds[1], (COLS, L), jnp.float32) ** block_levels(seeds[1], (COLS, L), ((0, 128), (1, 4)), -0.2, 0.2)), 0.19921875, 2.0).astype(jnp.bfloat16)
    condensate_optic = jnp.clip(jnp.exp(math.log(1.0) - 4.61031033 * jax.random.uniform(seeds[2], (COLS, L), jnp.float32) ** block_levels(seeds[2], (COLS, L), ((0, 128), (1, 4)), -0.2, 0.2)), 0.0099487305, 1.0).astype(jnp.bfloat16)
    sun_height_factor = draw_sun_height_factor(jax.random.fold_in(seeds[9], 71), 0)
    group_assignment = draw_group_assignment(jax.random.fold_in(seeds[9], 71), 0)
    opacity_factor = jnp.clip(jnp.exp(math.log(0.03) - 3.4011973 * jax.random.uniform(seeds[5], (GPOINT_NUMBER,), jnp.float32) ** block_levels(seeds[5], (GPOINT_NUMBER,), ((0, 4),), -0.2, 0.2)), 0.001, 0.03)
    thermal_power = jnp.clip(jax.random.uniform(seeds[6], (GPOINT_NUMBER,), jnp.float32, -2.0, 2.0) * block_levels(seeds[6], (GPOINT_NUMBER,), ((0, 4),), -0.4, 0.0), -2.0, 2.0)
    sunlight_weights = draw_sunlight_weights(jax.random.fold_in(seeds[9], 71), 0)
    thermal_weights = draw_thermal_weights(jax.random.fold_in(seeds[9], 71), 0)
    return dict(thermal_deviation=thermal_deviation, moisture_mass=moisture_mass, condensate_optic=condensate_optic, sun_height_factor=sun_height_factor, group_assignment=group_assignment, opacity_factor=opacity_factor, thermal_power=thermal_power, sunlight_weights=sunlight_weights, thermal_weights=thermal_weights)


def optical_depths(t, w, c, solar_elevation_factor, coefficient_entry, planck_entry, sunlight_entry, physics_entry):
    tau = coefficient_entry[:, None, None] * (w[None] * jnp.exp(planck_entry[:, None, None] * t[None]) + c[None])
    depth = 1.66 * jnp.cumsum(tau, axis=2)
    trans = jnp.exp(-depth)
    ones_col = jnp.ones(trans.shape[:2] + (1,), jnp.float32)
    above = jnp.concatenate([ones_col, trans[:, :, :-1]], axis=2)
    solar_part = sunlight_entry[:, None, None] * solar_elevation_factor[None, :, None] * (above - trans)
    emitted = physics_entry[:, None, None] * (1.0 + 0.2 * t[None]) * (1.0 - jnp.exp(-1.66 * tau))
    warming_rate = 0.0625 * jnp.sum(solar_part - emitted, axis=0)
    ground_flux = jnp.sum(sunlight_entry[:, None] * solar_elevation_factor[None, :] * trans[:, :, -1], axis=0)
    return warming_rate, ground_flux


def reference(thermal_deviation, moisture_mass, condensate_optic, sun_height_factor, group_assignment, opacity_factor, thermal_power, sunlight_weights, thermal_weights):
    per = COL_DEV // N_BLK
    order = jnp.argsort(group_assignment.reshape(N_BLK, COL_DEV), axis=1, stable=True).astype(jnp.int32)
    offsets = (jnp.arange(N_BLK, dtype=jnp.int32) * COL_DEV)[:, None]
    emitter_term = (order + offsets).reshape(N_BLK, N_BLK, per).transpose(1, 0, 2).reshape(-1)
    thermal_column = thermal_deviation[emitter_term].astype(jnp.float32)
    absorbing_mass = moisture_mass[emitter_term].astype(jnp.float32)
    condensate_field = condensate_optic.astype(jnp.float32)
    solar_elevation_factor = jnp.maximum(sun_height_factor, 0.0)
    group_sequence = GPOINT_NUMBER // 8

    def step(carry, radiative_settings):
        coefficient_entry, planck_entry, sunlight_entry, physics_entry = radiative_settings
        warming_rate, ground_flux = optical_depths(thermal_column, absorbing_mass, condensate_field, solar_elevation_factor, coefficient_entry, planck_entry, sunlight_entry, physics_entry)
        return (carry[0] + warming_rate, carry[1] + ground_flux), None

    start = (jnp.zeros((COLS, L), jnp.float32), jnp.zeros((COLS,), jnp.float32))
    radiative_settings = (opacity_factor.reshape(group_sequence, 8), thermal_power.reshape(group_sequence, 8), sunlight_weights.reshape(group_sequence, 8), thermal_weights.reshape(group_sequence, 8))
    (phys_heat, surface), unused = lax.scan(step, start, radiative_settings)
    heating = jnp.zeros((COLS, L), jnp.float32).at[emitter_term].set(phys_heat)
    return heating, surface
```

```python
import jax
import jax.numpy as jnp
from jax import lax
from jax.experimental import pallas as pl
from jax.experimental.pallas import tpu as pltpu
from jax.sharding import PartitionSpec as P

F32 = jnp.float32
BF16 = jnp.bfloat16
LOG2E = 1.4426950408889634
MESH = pl.DeviceIdType.MESH


def iota(shape, dim):
    return lax.broadcasted_iota(jnp.int32, shape, dim)


def split3(v):
    hi = v.astype(BF16)
    rest = v - hi.astype(F32)
    mid = rest.astype(BF16)
    lo = (rest - mid.astype(F32)).astype(BF16)
    return hi, mid, lo


def kernel(
    t_ref, w_ref, c_ref, mu_ref, g_ref, op_ref, tp_ref, sw_ref, tw_ref,
    heat_ref, surf_ref,
    scr_c, tx_c, rx_c, tx_g, rx_g, tx_h, rx_h, tx_s, rx_s,
    onehot, t_s, w_s, c_s, prm, acc,
    c_send, c_recv, g_send, g_recv, h_send, h_recv, s_send, s_recv,
):
    b = lax.axis_index("blk")
    a = lax.axis_index("ga")
    b_hi, b_lo = b // 32, b % 32
    mine = b_hi == a

    bar = pltpu.get_barrier_semaphore()

    def greet(dev):
        pl.semaphore_signal(bar, inc=1, device_id=dev, device_id_type=MESH)

    @pl.when(jnp.logical_not(mine))
    def _():
        greet((32 * a + b_lo, a))

    def greet_step(j, carry):
        greet((32 * a + (b_lo + j // 4) % 32, (a + j % 4) % 4))
        return carry

    lax.fori_loop(1, 128, greet_step, 0)
    for k in range(1, 4):
        greet((b, (a + k) % 4))

    scr_c[...] = c_ref[...].astype(F32)
    even = scr_c[pl.ds(0, 128, stride=2), :]
    odd = scr_c[pl.ds(1, 128, stride=2), :]
    mu_b = jnp.broadcast_to(jnp.maximum(mu_ref[...], 0.0), (128, 256))
    row, col = iota((128, 256), 0), iota((128, 256), 1)
    mu_0 = jnp.sum(jnp.where(col == 2 * row, mu_b, 0.0), axis=1, keepdims=True)
    mu_1 = jnp.sum(jnp.where(col == 2 * row + 1, mu_b, 0.0), axis=1, keepdims=True)
    msg = jnp.concatenate([even, odd, jnp.zeros((128, 64), F32)], axis=1)
    lane = iota((128, 128), 1)
    msg = jnp.where(lane == 64, mu_0, jnp.where(lane == 65, mu_1, msg))
    tx_c[:, 0, :] = msg

    grow = jnp.broadcast_to(g_ref[...].astype(F32), (256, 256))
    row, col = iota((256, 256), 0), iota((256, 256), 1)
    gcol = jnp.sum(jnp.where(row == col, grow, 0.0), axis=1, keepdims=True)
    second = jnp.sum(
        jnp.where(jnp.logical_and(grow == gcol, col < row), 1.0, 0.0), axis=1, keepdims=True
    )
    gi = gcol.astype(jnp.int32)
    place = (gi // 32) * 128 + second.astype(jnp.int32) * 32 + gi % 32
    n = iota((256, 512), 1)
    hot = jnp.where((n // 128) * 128 + n % 64 == place, 1.0, 0.0)
    onehot[...] = jnp.where(n % 128 < 64, hot, 0.0).astype(BF16)
    hot = hot.astype(BF16)
    for at, ref in ((0, t_ref), (32, w_ref)):
        moved = lax.dot_general(
            ref[...], hot, (((0,), (0,)), ((), ())), preferred_element_type=F32
        ).astype(BF16)
        for k in range(4):
            tx_g[k, at : at + 32, :] = moved[:, 128 * k : 128 * k + 128]

    prow, plane = iota((16, 128), 0), iota((16, 128), 1)
    tile = jnp.zeros((16, 128), F32)
    for j, ref in enumerate((op_ref, tp_ref, sw_ref, tw_ref)):
        v = ref[...]
        v = jnp.concatenate([v, v], axis=1)
        for s, part in enumerate(split3(v)):
            tile = jnp.where(prow == 3 * j + s, jnp.broadcast_to(part.astype(F32), (16, 128)), tile)
    tile = jnp.where(plane // 64 == a % 2, tile, 0.0).astype(BF16)
    for k in range(4):
        tx_g[k, 64:80, :] = tile

    pl.semaphore_wait(bar, jnp.where(mine, 130, 131))

    def c_copy(to):
        return pltpu.make_async_remote_copy(
            src_ref=tx_c.at[to],
            dst_ref=rx_c.at[a * 32 + b_lo],
            send_sem=c_send,
            recv_sem=c_recv,
            device_id=(to, b_hi),
            device_id_type=MESH,
        )

    def g_copy(k):
        to = (a + k) % 4
        return pltpu.make_async_remote_copy(
            src_ref=tx_g.at[to],
            dst_ref=rx_g.at[a],
            send_sem=g_send,
            recv_sem=g_recv,
            device_id=(b, to),
            device_id_type=MESH,
        )

    for k in range(1, 4):
        g_copy(k).start()

    @pl.when(mine)
    def _():
        pltpu.make_async_copy(tx_c.at[b], rx_c.at[a * 32 + b_lo], c_recv).start()

    @pl.when(jnp.logical_not(mine))
    def _():
        c_copy(b).start()

    def c_step(j, carry):
        c_copy((b + j) % 128).start()
        return carry

    lax.fori_loop(1, 128, c_step, 0)
    rx_g[a] = tx_g[a]

    def await_bytes(ref, sem):
        pltpu.make_async_copy(ref, ref, sem).wait()

    await_bytes(rx_g.at[pl.ds(0, 3)], g_recv)
    for k in range(4):
        t_s[32 * k : 32 * k + 32, :] = rx_g[k, 0:32, :].astype(F32)
        w_s[32 * k : 32 * k + 32, :] = rx_g[k, 32:64, :].astype(F32)
    parts = [rx_g[k, 64:80, :].astype(F32) for k in range(4)]
    parts = jnp.concatenate([parts[0] + parts[1], parts[2] + parts[3]], axis=0)
    m, n = iota((32, 512), 0), iota((32, 512), 1)
    pick = jnp.logical_and(
        m // 16 == (n % 128) // 64,
        jnp.logical_and((m % 16) // 3 == n // 128, m % 16 < 12),
    )
    pick = jnp.where(pick, 1.0, 0.0).astype(BF16)
    spread = lax.dot_general(
        jnp.transpose(parts).astype(BF16), pick, (((1,), (0,)), ((), ())),
        preferred_element_type=F32,
    )
    prm[0] = spread[:, 0:128] * (-1.66 * LOG2E)
    prm[1] = spread[:, 128:256] * LOG2E
    prm[2] = spread[:, 256:384]
    prm[3] = spread[:, 384:512]

    m, n = iota((256, 512), 0), iota((256, 512), 1)
    slot = m % 128
    pick = jnp.logical_and(slot // 32 == n // 128, n % 64 == (m // 128) * 32 + slot % 32)
    pick = jnp.where(pick, 1.0, 0.0).astype(BF16)
    await_bytes(rx_c, c_recv)
    got = jnp.transpose(rx_c[:, 0, :])
    both = jnp.concatenate([got[0:32], got[32:64]], axis=1).astype(BF16)
    cond = lax.dot_general(both, pick, (((1,), (0,)), ((), ())), preferred_element_type=F32)
    for k in range(4):
        c_s[32 * k : 32 * k + 32, :] = cond[:, 128 * k : 128 * k + 128]
    sun = got[64:72]
    lane = iota((1, 128), 1)
    sun = jnp.where(lane % 64 < 32, sun[0:1], pltpu.roll(sun, 32, 1)[1:2])
    sun = jnp.where(lane < 64, jnp.broadcast_to(sun, (8, 128)), 0.0)
    sun = sun + pltpu.roll(sun, 64, 1)

    def h_copy(to):
        return pltpu.make_async_remote_copy(
            src_ref=tx_h.at[to],
            dst_ref=rx_h.at[a],
            send_sem=h_send,
            recv_sem=h_recv,
            device_id=(b, to),
            device_id_type=MESH,
        )

    def level(k, trans):
        t = jnp.broadcast_to(t_s[pl.ds(k, 1), :], (8, 128))
        w = jnp.broadcast_to(w_s[pl.ds(k, 1), :], (8, 128))
        c = jnp.broadcast_to(c_s[pl.ds(k, 1), :], (8, 128))
        q = 1.0 + 0.2 * t
        total = None
        out = []
        for i in range(16):
            rows = slice(8 * i, 8 * i + 8)
            x = w * jnp.exp2(prm[1, rows, :] * t) + c
            e = jnp.exp2(prm[0, rows, :] * x)
            term = (1.0 - e) * (trans[i] - prm[3, rows, :] * q)
            out.append(trans[i] * e)
            total = term if total is None else total + term
        acc[k] = total
        return tuple(out)

    trans = tuple(prm[2, 8 * i : 8 * i + 8, :] * sun for i in range(16))
    for part in range(4):
        trans = lax.fori_loop(32 * part, 32 * part + 32, level, trans, unroll=2)
        heat = 0.0625 * jnp.sum(acc[32 * part : 32 * part + 32], axis=1)
        heat = heat + pltpu.roll(heat, 64, 1)

        @pl.when(a == part)
        def _():
            rx_h[part] = heat

        @pl.when(a != part)
        def _():
            tx_h[part] = heat
            h_copy(part).start()

    surf = trans[0]
    for i in range(1, 16):
        surf = surf + trans[i]
    surf = jnp.sum(surf, axis=0, keepdims=True)
    surf = jnp.broadcast_to(surf, (8, 128))
    surf = surf + pltpu.roll(surf, 64, 1)
    tx_s[0] = surf[0:1]

    def s_copy(j):
        return pltpu.make_async_remote_copy(
            src_ref=tx_s.at[0],
            dst_ref=rx_s.at[b_lo],
            send_sem=s_send,
            recv_sem=s_recv,
            device_id=(32 * a + (b_lo + j) % 32, b_hi),
            device_id_type=MESH,
        )

    @pl.when(mine)
    def _():
        pltpu.make_async_copy(tx_s.at[0], rx_s.at[b_lo], s_recv).start()

    @pl.when(jnp.logical_not(mine))
    def _():
        s_copy(0).start()

    def s_step(j, carry):
        s_copy(j).start()
        return carry

    lax.fori_loop(1, 32, s_step, 0)

    await_bytes(rx_h.at[pl.ds(0, 3)], h_recv)
    heat = jnp.concatenate([rx_h[k] for k in range(4)], axis=1)
    total = None
    for part in split3(heat):
        term = lax.dot_general(
            onehot[...], part, (((1,), (1,)), ((), ())), preferred_element_type=F32
        )
        total = term if total is None else total + term
    heat_ref[...] = total

    await_bytes(rx_s, s_recv)
    got = rx_s[:, 0, :]
    lane, row = iota((32, 128), 1), iota((32, 128), 0)
    first = jnp.sum(jnp.where(lane == b_lo, got, 0.0), axis=1, keepdims=True)
    second = jnp.sum(jnp.where(lane == 32 + b_lo, got, 0.0), axis=1, keepdims=True)
    rows = jnp.where(lane == 2 * row, first, jnp.where(lane == 2 * row + 1, second, 0.0))
    surf_ref[...] = jnp.sum(rows, axis=0, keepdims=True)[:, 0:64]

    await_bytes(tx_g.at[pl.ds(0, 3)], g_send)
    await_bytes(tx_h.at[pl.ds(0, 3)], h_send)

    @pl.when(mine)
    def _():
        await_bytes(tx_c.at[pl.ds(0, 127)], c_send)
        await_bytes(rx_s.at[pl.ds(0, 31)], s_send)

    @pl.when(jnp.logical_not(mine))
    def _():
        await_bytes(tx_c, c_send)
        await_bytes(rx_s, s_send)


def shards(
    thermal_deviation, moisture_mass, condensate_optic, sun_height_factor, group_assignment,
    opacity_factor, thermal_power, sunlight_weights, thermal_weights,
):
    vmem = pl.BlockSpec(memory_space=pltpu.VMEM)
    heating, surface = pl.pallas_call(
        kernel,
        out_shape=(
            jax.ShapeDtypeStruct((256, 32), F32),
            jax.ShapeDtypeStruct((1, 64), F32),
        ),
        in_specs=[vmem] * 9,
        out_specs=(vmem, vmem),
        scratch_shapes=[
            pltpu.VMEM((256, 32), F32),
            pltpu.VMEM((128, 1, 128), F32),
            pltpu.VMEM((128, 1, 128), F32),
            pltpu.VMEM((4, 80, 128), BF16),
            pltpu.VMEM((4, 80, 128), BF16),
            pltpu.VMEM((4, 32, 128), F32),
            pltpu.VMEM((4, 32, 128), F32),
            pltpu.VMEM((1, 1, 128), F32),
            pltpu.VMEM((32, 1, 128), F32),
            pltpu.VMEM((256, 512), BF16),
            pltpu.VMEM((128, 128), F32),
            pltpu.VMEM((128, 128), F32),
            pltpu.VMEM((128, 128), F32),
            pltpu.VMEM((4, 128, 128), F32),
            pltpu.VMEM((128, 8, 128), F32),
        ]
        + [pltpu.SemaphoreType.DMA] * 8,
        compiler_params=pltpu.CompilerParams(
            collective_id=0, has_side_effects=True, vmem_limit_bytes=24 * 1024 * 1024
        ),
    )(
        thermal_deviation,
        moisture_mass,
        condensate_optic,
        sun_height_factor.reshape(1, -1),
        group_assignment.reshape(1, -1),
        opacity_factor.reshape(1, -1),
        thermal_power.reshape(1, -1),
        sunlight_weights.reshape(1, -1),
        thermal_weights.reshape(1, -1),
    )
    return heating, surface.reshape(-1)


def solution(mesh):
    in_specs = (
        P("blk", "ga"), P("blk", "ga"), P("blk", "ga"), P("blk"), P("blk"),
        P("ga"), P("ga"), P("ga"), P("ga"),
    )
    out_specs = (P("blk", "ga"), P(("blk", "ga")))
    return jax.shard_map(shards, mesh=mesh, in_specs=in_specs, out_specs=out_specs, check_vma=False)
```

```python
import jax
import jax.numpy as jnp
from jax import lax
from jax.experimental import pallas as pl
from jax.experimental.pallas import tpu as pltpu
from jax.sharding import PartitionSpec as P

F32 = jnp.float32
BF16 = jnp.bfloat16
LOG2E = 1.4426950408889634
MESH = pl.DeviceIdType.MESH


def iota(shape, dim):
    return lax.broadcasted_iota(jnp.int32, shape, dim)


def split3(v):
    hi = v.astype(BF16)
    rest = v - hi.astype(F32)
    mid = rest.astype(BF16)
    lo = (rest - mid.astype(F32)).astype(BF16)
    return hi, mid, lo


def dot(x, y, dims):
    return lax.dot_general(x, y, (dims, ((), ())), preferred_element_type=F32)


def ones_where(cond):
    return jnp.where(cond, 1.0, 0.0).astype(BF16)


def kernel(
    t_hbm, w_hbm, c_hbm, mu_hbm, g_hbm, op_hbm, tp_hbm, sw_hbm, tw_hbm,
    heat_ref, surf_ref,
    t_in, w_in, c_in, mu_in, g_in, op_in, tp_in, sw_in, tw_in,
    tx_c, rx_c, tx_g, rx_g, tx_h, rx_h, tx_s, rx_s,
    onehot, t_s, w_s, c_s, prm, acc, xs,
    in_sem, c_send, c_recv, g_send, g_recv, h_send, h_recv, s_send, s_recv,
):
    b = lax.axis_index("blk")
    a = lax.axis_index("ga")
    b_hi, b_lo = b >> 5, b & 31
    mine = b_hi == a

    loads = [
        pltpu.make_async_copy(src, dst, in_sem.at[i])
        for i, (src, dst) in enumerate(
            (
                (c_hbm, c_in), (mu_hbm, mu_in), (g_hbm, g_in), (t_hbm, t_in), (w_hbm, w_in),
                (op_hbm, op_in), (tp_hbm, tp_in), (sw_hbm, sw_in), (tw_hbm, tw_in),
            )
        )
    ]
    for load in loads:
        load.start()

    bar = pltpu.get_barrier_semaphore()

    def greet(dev):
        pl.semaphore_signal(bar, inc=1, device_id=dev, device_id_type=MESH)

    for k in range(1, 4):
        greet((b, (a + k) & 3))

    @pl.when(jnp.logical_not(mine))
    def _():
        greet((32 * a + b_lo, a))

    def greet_step(j, carry):
        greet((32 * a + ((b_lo + (j >> 2)) & 31), (a + j) & 3))
        return carry

    lax.fori_loop(1, 128, greet_step, 0, unroll=8)

    loads[0].wait()
    loads[1].wait()
    c_t = c_in[...]
    sun_row = jnp.maximum(mu_in[...], 0.0)
    row, col = iota((16, 512), 0), iota((16, 512), 1)
    sun_two = jnp.broadcast_to(jnp.concatenate([sun_row, sun_row], axis=1), (16, 512))
    sun_tile = jnp.zeros((16, 512), F32)
    for s, part in enumerate(split3(sun_two)):
        sun_tile = jnp.where(row == 3 * (col >> 8) + s, part.astype(F32), sun_tile)
    none = jnp.zeros((32, 256), BF16)
    laid = jnp.concatenate(
        [
            jnp.concatenate([c_t, none], axis=1),
            jnp.concatenate([none, c_t], axis=1),
            sun_tile.astype(BF16),
            jnp.zeros((48, 512), BF16),
        ],
        axis=0,
    )
    row, col = iota((128, 512), 0), iota((128, 512), 1)
    pick = ones_where((col & 255) == 2 * row + (col >> 8))
    tx_c[:, 0, :] = dot(pick, laid, ((1,), (1,)))

    loads[2].wait()
    groups = g_in[...]
    member = groups == iota((128, 256), 0)
    earlier = ones_where(iota((256, 256), 0) < iota((256, 256), 1))
    before = dot(ones_where(member), earlier, ((1,), (0,)))
    second = jnp.sum(jnp.where(member, before, 0.0), axis=0, keepdims=True).astype(jnp.int32)
    place = (groups >> 5) * 128 + second * 32 + (groups & 31)
    n = iota((512, 256), 0)
    hot = ones_where((n & 447) == place)
    onehot[...] = hot
    loads[3].wait()
    loads[4].wait()
    moved = dot(jnp.concatenate([t_in[...], w_in[...]], axis=0), hot, ((1,), (1,))).astype(BF16)
    for k in range(4):
        tx_g[k, 0:64, :] = moved[:, 128 * k : 128 * k + 128]

    for load in loads[5:]:
        load.wait()
    row, lane = iota((16, 128), 0), iota((16, 128), 1)
    tile = jnp.zeros((16, 128), F32)
    for j, ref in enumerate((op_in, tp_in, sw_in, tw_in)):
        v = ref[...]
        v = jnp.broadcast_to(jnp.concatenate([v, v], axis=1), (16, 128))
        for s, part in enumerate(split3(v)):
            tile = jnp.where(row == 3 * j + s, part.astype(F32), tile)
    tile = jnp.where((lane >> 6) == (a & 1), tile, 0.0)
    c_sum = jnp.sum(c_t.astype(F32), axis=0, keepdims=True)
    for k in range(2):
        v = jnp.broadcast_to(c_sum[:, 128 * k : 128 * k + 128], (16, 128))
        full = tile
        for s, part in enumerate(split3(v)):
            full = jnp.where(row == 12 + s, part.astype(F32), full)
        for half in range(2):
            tx_g[2 * k + half, 64:80, :] = full.astype(BF16)

    pl.semaphore_wait(bar, jnp.where(mine, 130, 131))

    def c_copy(to):
        return pltpu.make_async_remote_copy(
            src_ref=tx_c.at[to],
            dst_ref=rx_c.at[a * 32 + b_lo],
            send_sem=c_send,
            recv_sem=c_recv,
            device_id=(to, b_hi),
            device_id_type=MESH,
        )

    def g_copy(k):
        to = (a + k) & 3
        return pltpu.make_async_remote_copy(
            src_ref=tx_g.at[to],
            dst_ref=rx_g.at[a],
            send_sem=g_send,
            recv_sem=g_recv,
            device_id=(b, to),
            device_id_type=MESH,
        )

    for k in range(1, 4):
        g_copy(k).start()

    @pl.when(mine)
    def _():
        pltpu.make_async_copy(tx_c.at[b], rx_c.at[a * 32 + b_lo], c_recv).start()

    @pl.when(jnp.logical_not(mine))
    def _():
        c_copy(b).start()

    def c_step(j, carry):
        c_copy((b + j) & 127).start()
        return carry

    lax.fori_loop(1, 128, c_step, 0, unroll=8)
    rx_g[a] = tx_g[a]

    def await_bytes(ref, sem):
        pltpu.make_async_copy(ref, ref, sem).wait()

    await_bytes(rx_g.at[pl.ds(0, 3)], g_recv)
    for k in range(4):
        t_s[32 * k : 32 * k + 32, :] = rx_g[k, 0:32, :].astype(F32)
        w_s[32 * k : 32 * k + 32, :] = rx_g[k, 32:64, :].astype(F32)
    parts = [rx_g[k, 64:80, :].astype(F32) for k in range(4)]
    parts = [parts[0] + parts[1], parts[2] + parts[3]]
    m, n = iota((32, 512), 0), iota((32, 512), 1)
    pick = jnp.logical_and(
        (m >> 4) == ((n & 127) >> 6),
        jnp.logical_and((m & 15) // 3 == (n >> 7), (m & 15) < 12),
    )
    spread = dot(
        jnp.transpose(jnp.concatenate(parts, axis=0)).astype(BF16), ones_where(pick), ((1,), (0,))
    )
    prm[0] = spread[:, 0:128] * (-1.66 * LOG2E)
    prm[1] = spread[:, 128:256] * LOG2E
    prm[2] = spread[:, 256:384]
    prm[3] = spread[:, 384:512]

    def absorb(k, sums):
        t = jnp.broadcast_to(t_s[pl.ds(k, 1), :], (8, 128))
        w = jnp.broadcast_to(w_s[pl.ds(k, 1), :], (8, 128))
        out = []
        for i in range(16):
            x = w * jnp.exp2(prm[1, 8 * i : 8 * i + 8, :] * t)
            xs[k, 8 * i : 8 * i + 8, :] = x
            out.append(sums[i] + x)
        return tuple(out)

    sums = lax.fori_loop(
        0, 128, absorb, tuple(jnp.zeros((8, 128), F32) for i in range(16)), unroll=2
    )

    sums = jnp.transpose(jnp.concatenate(sums, axis=0))
    for k in range(4):
        tx_s[:, k, :] = sums[32 * k : 32 * k + 32]

    def s_copy(j):
        to = (b_lo + j) & 31
        return pltpu.make_async_remote_copy(
            src_ref=tx_s.at[to],
            dst_ref=rx_s.at[b_lo],
            send_sem=s_send,
            recv_sem=s_recv,
            device_id=(32 * a + to, b_hi),
            device_id_type=MESH,
        )

    @pl.when(mine)
    def _():
        pltpu.make_async_copy(tx_s.at[b_lo], rx_s.at[b_lo], s_recv).start()

    @pl.when(jnp.logical_not(mine))
    def _():
        s_copy(0).start()

    def s_step(j, carry):
        s_copy(j).start()
        return carry

    lax.fori_loop(1, 32, s_step, 0, unroll=4)

    m, n = iota((256, 512), 0), iota((256, 512), 1)
    slot = m & 127
    pick = jnp.logical_and((slot >> 5) == (n >> 7), (n & 63) == (m >> 7) * 32 + (slot & 31))
    pick = ones_where(pick)
    await_bytes(rx_c, c_recv)
    got = jnp.transpose(rx_c[:, 0, :])
    both = jnp.concatenate([got[0:32], got[32:64]], axis=1).astype(BF16)
    cond = dot(both, pick, ((1,), (0,)))
    for k in range(4):
        c_s[32 * k : 32 * k + 32, :] = cond[:, 128 * k : 128 * k + 128]
    sun = got[64:72]
    first = sun[0:1] + sun[1:2] + sun[2:3]
    second = jnp.broadcast_to(sun[3:4] + sun[4:5] + sun[5:6], (8, 128))
    lane = iota((8, 128), 1)
    sun = jnp.where((lane & 63) < 32, jnp.broadcast_to(first, (8, 128)), pltpu.roll(second, 32, 1))
    sun = jnp.where(lane < 64, sun, 0.0)
    sun = sun + pltpu.roll(sun, 64, 1)

    def h_copy(to):
        return pltpu.make_async_remote_copy(
            src_ref=tx_h.at[to],
            dst_ref=rx_h.at[a],
            send_sem=h_send,
            recv_sem=h_recv,
            device_id=(b, to),
            device_id_type=MESH,
        )

    def level(k, trans):
        q = jnp.broadcast_to(1.0 + 0.2 * t_s[pl.ds(k, 1), :], (8, 128))
        c = jnp.broadcast_to(c_s[pl.ds(k, 1), :], (8, 128))
        total = None
        out = []
        for i in range(16):
            rows = slice(8 * i, 8 * i + 8)
            e = jnp.exp2(prm[0, rows, :] * (xs[k, rows, :] + c))
            term = (1.0 - e) * (trans[i] - prm[3, rows, :] * q)
            out.append(trans[i] * e)
            total = term if total is None else total + term
        acc[k] = total
        return tuple(out)

    trans = tuple(prm[2, 8 * i : 8 * i + 8, :] * sun for i in range(16))
    for part in range(4):
        trans = lax.fori_loop(32 * part, 32 * part + 32, level, trans, unroll=2)
        heat = 0.0625 * jnp.sum(acc[32 * part : 32 * part + 32], axis=1)
        heat = heat + pltpu.roll(heat, 64, 1)

        @pl.when(a == part)
        def _():
            rx_h[part] = heat

        @pl.when(a != part)
        def _():
            tx_h[part] = heat
            h_copy(part).start()

    await_bytes(rx_s, s_recv)
    lane, row = iota((32, 128), 1), iota((32, 128), 0)
    c_all = jnp.broadcast_to(
        jnp.sum(parts[0][12:15] + parts[1][12:15], axis=0, keepdims=True), (32, 128)
    )
    mu_all = jnp.broadcast_to(mu_in[...], (32, 256))
    lane2, row2 = iota((32, 256), 1), iota((32, 256), 0)
    rows = None
    for r in range(2):
        at = 2 * row + r
        c_col = jnp.sum(jnp.where(lane == (a & 1) * 64 + at, c_all, 0.0), axis=1, keepdims=True)
        mu_col = jnp.sum(
            jnp.where(lane2 == a * 64 + 2 * row2 + r, mu_all, 0.0), axis=1, keepdims=True
        )
        flux = None
        for half in range(2):
            par = parts[half]
            factor = jnp.sum(par[0:3], axis=0, keepdims=True) * (-1.66 * LOG2E)
            weight = jnp.sum(par[6:9], axis=0, keepdims=True)
            term = weight * jnp.exp2(factor * (rx_s[:, 2 * half + r, :] + c_col))
            flux = term if flux is None else flux + term
        flux = jnp.sum(flux, axis=1, keepdims=True) * jnp.maximum(mu_col, 0.0)
        flux = jnp.where(lane == at, flux, 0.0)
        rows = flux if rows is None else rows + flux
    surf_ref[...] = jnp.sum(rows, axis=0, keepdims=True)[:, 0:64]

    await_bytes(rx_h.at[pl.ds(0, 3)], h_recv)
    heat = jnp.concatenate([rx_h[k] for k in range(4)], axis=1)
    heat = jnp.where((iota((32, 512), 1) & 127) < 64, heat, 0.0)
    heat = dot(jnp.concatenate(split3(heat), axis=0), onehot[...], ((1,), (0,)))
    heat_ref[...] = heat[0:32] + heat[32:64] + heat[64:96]

    await_bytes(tx_g.at[pl.ds(0, 3)], g_send)
    await_bytes(tx_h.at[pl.ds(0, 3)], h_send)

    @pl.when(mine)
    def _():
        await_bytes(tx_c.at[pl.ds(0, 127)], c_send)
        await_bytes(tx_s.at[pl.ds(0, 31)], s_send)

    @pl.when(jnp.logical_not(mine))
    def _():
        await_bytes(tx_c, c_send)
        await_bytes(tx_s, s_send)


def shards(
    thermal_deviation, moisture_mass, condensate_optic, sun_height_factor, group_assignment,
    opacity_factor, thermal_power, sunlight_weights, thermal_weights,
):
    vmem = pl.BlockSpec(memory_space=pltpu.VMEM)
    heating, surface = pl.pallas_call(
        kernel,
        out_shape=(
            jax.ShapeDtypeStruct((32, 256), F32),
            jax.ShapeDtypeStruct((1, 64), F32),
        ),
        in_specs=[pl.BlockSpec(memory_space=pltpu.HBM)] * 9,
        out_specs=(vmem, vmem),
        scratch_shapes=[
            pltpu.VMEM((32, 256), BF16),
            pltpu.VMEM((32, 256), BF16),
            pltpu.VMEM((32, 256), BF16),
            pltpu.VMEM((1, 256), F32),
            pltpu.VMEM((1, 256), jnp.int32),
            pltpu.VMEM((1, 64), F32),
            pltpu.VMEM((1, 64), F32),
            pltpu.VMEM((1, 64), F32),
            pltpu.VMEM((1, 64), F32),
            pltpu.VMEM((128, 1, 128), F32),
            pltpu.VMEM((128, 1, 128), F32),
            pltpu.VMEM((4, 80, 128), BF16),
            pltpu.VMEM((4, 80, 128), BF16),
            pltpu.VMEM((4, 32, 128), F32),
            pltpu.VMEM((4, 32, 128), F32),
            pltpu.VMEM((32, 4, 128), F32),
            pltpu.VMEM((32, 4, 128), F32),
            pltpu.VMEM((512, 256), BF16),
            pltpu.VMEM((128, 128), F32),
            pltpu.VMEM((128, 128), F32),
            pltpu.VMEM((128, 128), F32),
            pltpu.VMEM((4, 128, 128), F32),
            pltpu.VMEM((128, 8, 128), F32),
            pltpu.VMEM((128, 128, 128), F32),
            pltpu.SemaphoreType.DMA((9,)),
        ]
        + [pltpu.SemaphoreType.DMA] * 8,
        compiler_params=pltpu.CompilerParams(
            collective_id=0, has_side_effects=True, vmem_limit_bytes=60 * 1024 * 1024
        ),
    )(
        thermal_deviation.T,
        moisture_mass.T,
        condensate_optic.T,
        sun_height_factor.reshape(1, -1),
        group_assignment.reshape(1, -1),
        opacity_factor.reshape(1, -1),
        thermal_power.reshape(1, -1),
        sunlight_weights.reshape(1, -1),
        thermal_weights.reshape(1, -1),
    )
    return heating.T, surface.reshape(-1)


def solution(mesh):
    in_specs = (
        P("blk", "ga"), P("blk", "ga"), P("blk", "ga"), P("blk"), P("blk"),
        P("ga"), P("ga"), P("ga"), P("ga"),
    )
    out_specs = (P("blk", "ga"), P(("blk", "ga")))
    return jax.shard_map(shards, mesh=mesh, in_specs=in_specs, out_specs=out_specs, check_vma=False)
```

```python
import jax
import jax.numpy as jnp
from jax import lax
from jax.experimental import pallas as pl
from jax.experimental.pallas import tpu as pltpu
from jax.sharding import PartitionSpec as P

F32 = jnp.float32
BF16 = jnp.bfloat16
UNROLL = 8
LOG2E = 1.4426950408889634
MESH = pl.DeviceIdType.MESH


def iota(shape, dim):
    return lax.broadcasted_iota(jnp.int32, shape, dim)


def split3(v):
    hi = v.astype(BF16)
    rest = v - hi.astype(F32)
    mid = rest.astype(BF16)
    lo = (rest - mid.astype(F32)).astype(BF16)
    return hi, mid, lo


def dot(x, y, dims):
    return lax.dot_general(x, y, (dims, ((), ())), preferred_element_type=F32)


def ones_where(cond):
    return jnp.where(cond, 1.0, 0.0).astype(BF16)


def kernel(
    t_hbm, w_hbm, c_hbm, mu_hbm, g_hbm, op_hbm, tp_hbm, sw_hbm, tw_hbm,
    heat_ref, surf_ref,
    t_in, w_in, c_in, mu_in, g_in, op_in, tp_in, sw_in, tw_in,
    tx_c, rx_c, tx_g, rx_g, tx_h, rx_h, tx_s, rx_s,
    onehot, t_s, w_s, c_s, prm, acc, xs,
    in_sem, c_send, c_recv, g_send, g_recv, h_send, h_recv, s_send, s_recv,
):
    b = lax.axis_index("blk")
    a = lax.axis_index("ga")
    b_hi, b_lo = b >> 5, b & 31
    mine = b_hi == a

    loads = [
        pltpu.make_async_copy(src, dst, in_sem.at[i])
        for i, (src, dst) in enumerate(
            (
                (c_hbm, c_in), (mu_hbm, mu_in), (g_hbm, g_in), (t_hbm, t_in), (w_hbm, w_in),
                (op_hbm, op_in), (tp_hbm, tp_in), (sw_hbm, sw_in), (tw_hbm, tw_in),
            )
        )
    ]
    for load in loads:
        load.start()

    bar = pltpu.get_barrier_semaphore()

    def greet(dev):
        pl.semaphore_signal(bar, inc=1, device_id=dev, device_id_type=MESH)

    for k in range(1, 4):
        greet((b, (a + k) & 3))

    @pl.when(jnp.logical_not(mine))
    def _():
        greet((32 * a + b_lo, a))

    def greet_step(j, carry):
        greet((32 * a + ((b_lo + (j >> 2)) & 31), (a + j) & 3))
        return carry

    lax.fori_loop(1, 128, greet_step, 0, unroll=8)

    loads[0].wait()
    loads[1].wait()
    c_t = c_in[...]
    sun_row = jnp.maximum(mu_in[...], 0.0)
    row, col = iota((16, 512), 0), iota((16, 512), 1)
    sun_two = jnp.broadcast_to(jnp.concatenate([sun_row, sun_row], axis=1), (16, 512))
    sun_tile = jnp.zeros((16, 512), F32)
    for s, part in enumerate(split3(sun_two)):
        sun_tile = jnp.where(row == 3 * (col >> 8) + s, part.astype(F32), sun_tile)
    none = jnp.zeros((32, 256), BF16)
    laid = jnp.concatenate(
        [
            jnp.concatenate([c_t, none], axis=1),
            jnp.concatenate([none, c_t], axis=1),
            sun_tile.astype(BF16),
            jnp.zeros((48, 512), BF16),
        ],
        axis=0,
    )
    row, col = iota((128, 512), 0), iota((128, 512), 1)
    pick = ones_where((col & 255) == 2 * row + (col >> 8))
    tx_c[:, 0, :] = dot(pick, laid, ((1,), (1,)))

    loads[2].wait()
    groups = g_in[...]
    member = groups == iota((128, 256), 0)
    earlier = ones_where(iota((256, 256), 0) < iota((256, 256), 1))
    before = dot(ones_where(member), earlier, ((1,), (0,)))
    second = jnp.sum(jnp.where(member, before, 0.0), axis=0, keepdims=True).astype(jnp.int32)
    place = (groups >> 5) * 128 + second * 32 + (groups & 31)
    n = iota((512, 256), 0)
    hot = ones_where((n & 447) == place)
    onehot[...] = hot
    loads[3].wait()
    loads[4].wait()
    moved = dot(jnp.concatenate([t_in[...], w_in[...]], axis=0), hot, ((1,), (1,))).astype(BF16)
    for k in range(4):
        tx_g[k, 0:64, :] = moved[:, 128 * k : 128 * k + 128]

    for load in loads[5:]:
        load.wait()
    row, lane = iota((16, 128), 0), iota((16, 128), 1)
    tile = jnp.zeros((16, 128), F32)
    for j, ref in enumerate((op_in, tp_in, sw_in, tw_in)):
        v = ref[...]
        v = jnp.broadcast_to(jnp.concatenate([v, v], axis=1), (16, 128))
        for s, part in enumerate(split3(v)):
            tile = jnp.where(row == 3 * j + s, part.astype(F32), tile)
    tile = jnp.where((lane >> 6) == (a & 1), tile, 0.0)
    c_sum = jnp.sum(c_t.astype(F32), axis=0, keepdims=True)
    for k in range(2):
        v = jnp.broadcast_to(c_sum[:, 128 * k : 128 * k + 128], (16, 128))
        full = tile
        for s, part in enumerate(split3(v)):
            full = jnp.where(row == 12 + s, part.astype(F32), full)
        for half in range(2):
            tx_g[2 * k + half, 64:80, :] = full.astype(BF16)

    pl.semaphore_wait(bar, jnp.where(mine, 130, 131))

    def c_copy(to):
        return pltpu.make_async_remote_copy(
            src_ref=tx_c.at[to],
            dst_ref=rx_c.at[a * 32 + b_lo],
            send_sem=c_send,
            recv_sem=c_recv,
            device_id=(to, b_hi),
            device_id_type=MESH,
        )

    def g_copy(k):
        to = (a + k) & 3
        return pltpu.make_async_remote_copy(
            src_ref=tx_g.at[to],
            dst_ref=rx_g.at[a],
            send_sem=g_send,
            recv_sem=g_recv,
            device_id=(b, to),
            device_id_type=MESH,
        )

    for k in range(1, 4):
        g_copy(k).start()

    @pl.when(mine)
    def _():
        pltpu.make_async_copy(tx_c.at[b], rx_c.at[a * 32 + b_lo], c_recv).start()

    @pl.when(jnp.logical_not(mine))
    def _():
        c_copy(b).start()

    def c_step(j, carry):
        c_copy((b + j) & 127).start()
        return carry

    lax.fori_loop(1, 128, c_step, 0, unroll=8)
    rx_g[a] = tx_g[a]

    def await_bytes(ref, sem):
        pltpu.make_async_copy(ref, ref, sem).wait()

    await_bytes(rx_g.at[pl.ds(0, 3)], g_recv)
    for k in range(4):
        t_s[32 * k : 32 * k + 32, :] = rx_g[k, 0:32, :].astype(F32)
        w_s[32 * k : 32 * k + 32, :] = rx_g[k, 32:64, :].astype(F32)
    parts = [rx_g[k, 64:80, :].astype(F32) for k in range(4)]
    parts = [parts[0] + parts[1], parts[2] + parts[3]]
    m, n = iota((32, 512), 0), iota((32, 512), 1)
    pick = jnp.logical_and(
        (m >> 4) == ((n & 127) >> 6),
        jnp.logical_and((m & 15) // 3 == (n >> 7), (m & 15) < 12),
    )
    spread = dot(
        jnp.transpose(jnp.concatenate(parts, axis=0)).astype(BF16), ones_where(pick), ((1,), (0,))
    )
    prm[0] = spread[:, 0:128] * (-1.66 * LOG2E)
    prm[1] = spread[:, 128:256] * LOG2E
    prm[2] = spread[:, 256:384]
    prm[3] = spread[:, 384:512]

    power = [prm[1, 8 * i : 8 * i + 8, :] for i in range(16)]

    def absorb(k, sums):
        sums = list(sums)
        rows_t = [jnp.broadcast_to(t_s[pl.ds(4 * k + u, 1), :], (8, 128)) for u in range(4)]
        rows_w = [jnp.broadcast_to(w_s[pl.ds(4 * k + u, 1), :], (8, 128)) for u in range(4)]
        for u in range(4):
            for i in range(16):
                x = rows_w[u] * jnp.exp2(power[i] * rows_t[u])
                xs[4 * k + u, 8 * i : 8 * i + 8, :] = x
                sums[i] = sums[i] + x
        return tuple(sums)

    sums = lax.fori_loop(0, 32, absorb, tuple(jnp.zeros((8, 128), F32) for i in range(16)))

    sums = jnp.transpose(jnp.concatenate(sums, axis=0))
    for k in range(4):
        tx_s[:, k, :] = sums[32 * k : 32 * k + 32]

    def s_copy(j):
        to = (b_lo + j) & 31
        return pltpu.make_async_remote_copy(
            src_ref=tx_s.at[to],
            dst_ref=rx_s.at[b_lo],
            send_sem=s_send,
            recv_sem=s_recv,
            device_id=(32 * a + to, b_hi),
            device_id_type=MESH,
        )

    @pl.when(mine)
    def _():
        pltpu.make_async_copy(tx_s.at[b_lo], rx_s.at[b_lo], s_recv).start()

    @pl.when(jnp.logical_not(mine))
    def _():
        s_copy(0).start()

    def s_step(j, carry):
        s_copy(j).start()
        return carry

    lax.fori_loop(1, 32, s_step, 0, unroll=4)

    m, n = iota((256, 512), 0), iota((256, 512), 1)
    slot = m & 127
    pick = jnp.logical_and((slot >> 5) == (n >> 7), (n & 63) == (m >> 7) * 32 + (slot & 31))
    pick = ones_where(pick)
    await_bytes(rx_c, c_recv)
    got = jnp.transpose(rx_c[:, 0, :])
    both = jnp.concatenate([got[0:32], got[32:64]], axis=1).astype(BF16)
    cond = dot(both, pick, ((1,), (0,)))
    for k in range(4):
        c_s[32 * k : 32 * k + 32, :] = cond[:, 128 * k : 128 * k + 128]
    sun = got[64:72]
    first = sun[0:1] + sun[1:2] + sun[2:3]
    second = jnp.broadcast_to(sun[3:4] + sun[4:5] + sun[5:6], (8, 128))
    lane = iota((8, 128), 1)
    sun = jnp.where((lane & 63) < 32, jnp.broadcast_to(first, (8, 128)), pltpu.roll(second, 32, 1))
    sun = jnp.where(lane < 64, sun, 0.0)
    sun = sun + pltpu.roll(sun, 64, 1)

    def h_copy(to):
        return pltpu.make_async_remote_copy(
            src_ref=tx_h.at[to],
            dst_ref=rx_h.at[a],
            send_sem=h_send,
            recv_sem=h_recv,
            device_id=(b, to),
            device_id_type=MESH,
        )

    def levels(first, trans):
        rows_q = [
            jnp.broadcast_to(1.0 + 0.2 * t_s[pl.ds(first + u, 1), :], (8, 128)) for u in range(UNROLL)
        ]
        rows_c = [jnp.broadcast_to(c_s[pl.ds(first + u, 1), :], (8, 128)) for u in range(UNROLL)]
        totals = [None] * UNROLL
        trans = list(trans)
        for u in range(UNROLL):
            for i in range(16):
                rows = slice(8 * i, 8 * i + 8)
                e = jnp.exp2(prm[0, rows, :] * (xs[first + u, rows, :] + rows_c[u]))
                term = (1.0 - e) * (trans[i] - prm[3, rows, :] * rows_q[u])
                trans[i] = trans[i] * e
                totals[u] = term if i == 0 else totals[u] + term
        for u in range(UNROLL):
            acc[first + u] = totals[u]
        return tuple(trans)

    trans = tuple(prm[2, 8 * i : 8 * i + 8, :] * sun for i in range(16))
    def quarter(part, trans):
        first = pl.multiple_of(32 * part, 32)
        trans = lax.fori_loop(
            0, 32 // UNROLL, lambda k, v: levels(first + UNROLL * k, v), trans
        )
        heat = 0.0625 * jnp.sum(acc[pl.ds(first, 32)], axis=1)
        heat = heat + pltpu.roll(heat, 64, 1)

        @pl.when(a == part)
        def _():
            rx_h[part] = heat

        @pl.when(a != part)
        def _():
            tx_h[part] = heat
            h_copy(part).start()

        return trans

    lax.fori_loop(0, 4, quarter, trans)

    await_bytes(rx_s, s_recv)
    lane, row = iota((32, 128), 1), iota((32, 128), 0)
    c_all = jnp.broadcast_to(
        jnp.sum(parts[0][12:15] + parts[1][12:15], axis=0, keepdims=True), (32, 128)
    )
    mu_all = jnp.broadcast_to(mu_in[...], (32, 256))
    lane2, row2 = iota((32, 256), 1), iota((32, 256), 0)
    rows = None
    for r in range(2):
        at = 2 * row + r
        c_col = jnp.sum(jnp.where(lane == (a & 1) * 64 + at, c_all, 0.0), axis=1, keepdims=True)
        mu_col = jnp.sum(
            jnp.where(lane2 == a * 64 + 2 * row2 + r, mu_all, 0.0), axis=1, keepdims=True
        )
        flux = None
        for half in range(2):
            par = parts[half]
            factor = jnp.sum(par[0:3], axis=0, keepdims=True) * (-1.66 * LOG2E)
            weight = jnp.sum(par[6:9], axis=0, keepdims=True)
            term = weight * jnp.exp2(factor * (rx_s[:, 2 * half + r, :] + c_col))
            flux = term if flux is None else flux + term
        flux = jnp.sum(flux, axis=1, keepdims=True) * jnp.maximum(mu_col, 0.0)
        flux = jnp.where(lane == at, flux, 0.0)
        rows = flux if rows is None else rows + flux
    surf_ref[...] = jnp.sum(rows, axis=0, keepdims=True)[:, 0:64]

    await_bytes(rx_h.at[pl.ds(0, 3)], h_recv)
    heat = jnp.concatenate([rx_h[k] for k in range(4)], axis=1)
    heat = jnp.where((iota((32, 512), 1) & 127) < 64, heat, 0.0)
    heat = dot(jnp.concatenate(split3(heat), axis=0), onehot[...], ((1,), (0,)))
    heat_ref[...] = heat[0:32] + heat[32:64] + heat[64:96]

    await_bytes(tx_g.at[pl.ds(0, 3)], g_send)
    await_bytes(tx_h.at[pl.ds(0, 3)], h_send)

    @pl.when(mine)
    def _():
        await_bytes(tx_c.at[pl.ds(0, 127)], c_send)
        await_bytes(tx_s.at[pl.ds(0, 31)], s_send)

    @pl.when(jnp.logical_not(mine))
    def _():
        await_bytes(tx_c, c_send)
        await_bytes(tx_s, s_send)


def place(heat_in, surf_in, heat_out, surf_out, sem):
    copies = [
        pltpu.make_async_copy(heat_in, heat_out, sem.at[0]),
        pltpu.make_async_copy(surf_in, surf_out, sem.at[1]),
    ]
    for copy in copies:
        copy.start()
    for copy in copies:
        copy.wait()


def shards(
    thermal_deviation, moisture_mass, condensate_optic, sun_height_factor, group_assignment,
    opacity_factor, thermal_power, sunlight_weights, thermal_weights,
):
    vmem = pl.BlockSpec(memory_space=pltpu.VMEM)
    heating, surface = pl.pallas_call(
        kernel,
        out_shape=(
            jax.ShapeDtypeStruct((32, 256), F32),
            jax.ShapeDtypeStruct((1, 64), F32),
        ),
        in_specs=[pl.BlockSpec(memory_space=pltpu.HBM)] * 9,
        out_specs=(vmem, vmem),
        scratch_shapes=[
            pltpu.VMEM((32, 256), BF16),
            pltpu.VMEM((32, 256), BF16),
            pltpu.VMEM((32, 256), BF16),
            pltpu.VMEM((1, 256), F32),
            pltpu.VMEM((1, 256), jnp.int32),
            pltpu.VMEM((1, 64), F32),
            pltpu.VMEM((1, 64), F32),
            pltpu.VMEM((1, 64), F32),
            pltpu.VMEM((1, 64), F32),
            pltpu.VMEM((128, 1, 128), F32),
            pltpu.VMEM((128, 1, 128), F32),
            pltpu.VMEM((4, 80, 128), BF16),
            pltpu.VMEM((4, 80, 128), BF16),
            pltpu.VMEM((4, 32, 128), F32),
            pltpu.VMEM((4, 32, 128), F32),
            pltpu.VMEM((32, 4, 128), F32),
            pltpu.VMEM((32, 4, 128), F32),
            pltpu.VMEM((512, 256), BF16),
            pltpu.VMEM((128, 128), F32),
            pltpu.VMEM((128, 128), F32),
            pltpu.VMEM((128, 128), F32),
            pltpu.VMEM((4, 128, 128), F32),
            pltpu.VMEM((128, 8, 128), F32),
            pltpu.VMEM((128, 128, 128), F32),
            pltpu.SemaphoreType.DMA((9,)),
        ]
        + [pltpu.SemaphoreType.DMA] * 8,
        compiler_params=pltpu.CompilerParams(
            collective_id=0, has_side_effects=True, vmem_limit_bytes=32 * 1024 * 1024
        ),
    )(
        *(
            pltpu.with_memory_space_constraint(v, pltpu.HBM)
            for v in (
                thermal_deviation.T,
                moisture_mass.T,
                condensate_optic.T,
                sun_height_factor.reshape(1, -1),
                group_assignment.reshape(1, -1),
                opacity_factor.reshape(1, -1),
                thermal_power.reshape(1, -1),
                sunlight_weights.reshape(1, -1),
                thermal_weights.reshape(1, -1),
            )
        )
    )
    heating, surface = pl.pallas_call(
        place,
        out_shape=(
            jax.ShapeDtypeStruct((32, 256), F32),
            jax.ShapeDtypeStruct((1, 64), F32),
        ),
        in_specs=[vmem] * 2,
        out_specs=[pl.BlockSpec(memory_space=pltpu.HBM)] * 2,
        scratch_shapes=[pltpu.SemaphoreType.DMA((2,))],
    )(*(pltpu.with_memory_space_constraint(v, pltpu.VMEM) for v in (heating, surface)))
    return heating.T, surface.reshape(-1)


def solution(mesh):
    in_specs = (
        P("blk", "ga"), P("blk", "ga"), P("blk", "ga"), P("blk"), P("blk"),
        P("ga"), P("ga"), P("ga"), P("ga"),
    )
    out_specs = (P("blk", "ga"), P(("blk", "ga")))
    return jax.shard_map(shards, mesh=mesh, in_specs=in_specs, out_specs=out_specs, check_vma=False)
```

```python
import jax
import jax.numpy as jnp
from jax import lax
from jax.experimental import pallas as pl
from jax.experimental.pallas import tpu as pltpu
from jax.sharding import PartitionSpec as P

F32 = jnp.float32
BF16 = jnp.bfloat16
UNROLL = 8
LOG2E = 1.4426950408889634
MESH = pl.DeviceIdType.MESH


def iota(shape, dim):
    return lax.broadcasted_iota(jnp.int32, shape, dim)


def split3(v):
    hi = v.astype(BF16)
    rest = v - hi.astype(F32)
    mid = rest.astype(BF16)
    lo = (rest - mid.astype(F32)).astype(BF16)
    return hi, mid, lo


def dot(x, y, dims):
    return lax.dot_general(x, y, (dims, ((), ())), preferred_element_type=F32)


def ones_where(cond):
    return jnp.where(cond, 1.0, 0.0).astype(BF16)


EARLY, LATE = 72, 56


def is_late(blk):
    return jnp.logical_or(blk >= 96, jnp.logical_and(blk >= 64, (blk & 15) >= 4))


def early_blk(j):
    return jnp.where(j >= 68, j + 12, j)


def late_blk(j):
    return jnp.where(j >= 12, j + 72, j + 68)


def kernel(
    t_hbm, w_hbm, c_hbm, mu_hbm, g_hbm, op_hbm, tp_hbm, sw_hbm, tw_hbm,
    heat_ref, surf_ref,
    t_in, w_in, c_in, mu_in, g_in, op_in, tp_in, sw_in, tw_in,
    tx_c, rx_c, tx_g, rx_g, tx_h, rx_h, tx_s, rx_s,
    onehot, t_s, w_s, c_s, prm, acc, xs,
    in_sem, c_send, c_recv, g_send, g_recv, h_send, h_recv, s_send, s_recv, pair_sem,
):
    b = lax.axis_index("blk")
    a = lax.axis_index("ga")
    b_hi, b_lo = b >> 5, b & 31
    mine = b_hi == a
    core = b & 1
    late = is_late(b)
    sibling = (b ^ 1, a)

    loads = [
        pltpu.make_async_copy(src, dst, in_sem.at[i])
        for i, (src, dst) in enumerate(
            (
                (c_hbm, c_in), (mu_hbm, mu_in), (g_hbm, g_in), (t_hbm, t_in), (w_hbm, w_in),
                (op_hbm, op_in), (tp_hbm, tp_in), (sw_hbm, sw_in), (tw_hbm, tw_in),
            )
        )
    ]
    for load in loads:
        load.start()

    bar = pltpu.get_barrier_semaphore()

    def greet(dev):
        pl.semaphore_signal(bar, inc=1, device_id=dev, device_id_type=MESH)

    greet(sibling)
    for k in range(1, 4):
        greet((b & 126, (a + k) & 3))
    told = jnp.where(late, 1, 0)
    told_self = jnp.logical_and(mine, core == told)

    def announce(j):
        greet((32 * a + ((b_lo + (j >> 2) * 2) & 30) + told, (a + j) & 3))

    @pl.when(jnp.logical_not(told_self))
    def _():
        announce(0)

    def announce_step(j, carry):
        announce(j)
        return carry

    lax.fori_loop(1, 64, announce_step, 0, unroll=7)

    loads[0].wait()
    loads[1].wait()
    c_t = c_in[...]
    sun_row = jnp.maximum(mu_in[...], 0.0)
    row, col = iota((16, 512), 0), iota((16, 512), 1)
    sun_two = jnp.broadcast_to(jnp.concatenate([sun_row, sun_row], axis=1), (16, 512))
    sun_tile = jnp.zeros((16, 512), F32)
    for s, part in enumerate(split3(sun_two)):
        sun_tile = jnp.where(row == 3 * (col >> 8) + s, part.astype(F32), sun_tile)
    none = jnp.zeros((32, 256), BF16)
    laid = jnp.concatenate(
        [
            jnp.concatenate([c_t, none], axis=1),
            jnp.concatenate([none, c_t], axis=1),
            sun_tile.astype(BF16),
            jnp.zeros((48, 512), BF16),
        ],
        axis=0,
    )
    row, col = iota((128, 512), 0), iota((128, 512), 1)
    pick = ones_where((col & 255) == 2 * row + (col >> 8))
    tx_c[:, 0, :] = dot(pick, laid, ((1,), (1,)))

    loads[2].wait()
    groups = g_in[...]
    member = groups == iota((128, 256), 0)
    earlier = ones_where(iota((256, 256), 0) < iota((256, 256), 1))
    before = dot(ones_where(member), earlier, ((1,), (0,)))
    second = jnp.sum(jnp.where(member, before, 0.0), axis=0, keepdims=True).astype(jnp.int32)
    place = (groups >> 5) * 128 + second * 32 + (groups & 31)
    n = iota((512, 256), 0)
    hot = ones_where((n & 447) == place)
    onehot[...] = hot
    loads[3].wait()
    loads[4].wait()
    moved = dot(jnp.concatenate([t_in[...], w_in[...]], axis=0), hot, ((1,), (1,))).astype(BF16)
    for k in range(4):
        tx_g[k, 0:64, :] = moved[:, 128 * k : 128 * k + 128]

    for load in loads[5:]:
        load.wait()
    row, lane = iota((16, 128), 0), iota((16, 128), 1)
    tile = jnp.zeros((16, 128), F32)
    for j, ref in enumerate((op_in, tp_in, sw_in, tw_in)):
        v = ref[...]
        v = jnp.broadcast_to(jnp.concatenate([v, v], axis=1), (16, 128))
        for s, part in enumerate(split3(v)):
            tile = jnp.where(row == 3 * j + s, part.astype(F32), tile)
    tile = jnp.where((lane >> 6) == (a & 1), tile, 0.0)
    c_sum = jnp.sum(c_t.astype(F32), axis=0, keepdims=True)
    for k in range(2):
        v = jnp.broadcast_to(c_sum[:, 128 * k : 128 * k + 128], (16, 128))
        full = tile
        for s, part in enumerate(split3(v)):
            full = jnp.where(row == 12 + s, part.astype(F32), full)
        for half in range(2):
            tx_g[2 * k + half, 64:80, :] = full.astype(BF16)

    self_counted = jnp.where(told_self, 1, 0)

    @pl.when(core == 0)
    def _():
        pl.semaphore_wait(bar, EARLY + 7 - self_counted)
        pl.semaphore_signal(pair_sem, inc=1, device_id=sibling, device_id_type=MESH)

    @pl.when(core == 1)
    def _():
        pl.semaphore_wait(pair_sem, 1)

    def c_copy(to):
        return pltpu.make_async_remote_copy(
            src_ref=tx_c.at[to],
            dst_ref=rx_c.at[a * 32 + b_lo],
            send_sem=c_send,
            recv_sem=c_recv,
            device_id=(to, b_hi),
            device_id_type=MESH,
        )

    def g_copy(k):
        to = (a + k) & 3
        return pltpu.make_async_remote_copy(
            src_ref=tx_g.at[to],
            dst_ref=rx_g.at[a],
            send_sem=g_send,
            recv_sem=g_recv,
            device_id=(b, to),
            device_id_type=MESH,
        )

    for k in range(1, 4):
        g_copy(k).start()

    @pl.when(mine)
    def _():
        pltpu.make_async_copy(tx_c.at[b], rx_c.at[a * 32 + b_lo], c_recv).start()

    early_first = jnp.where(late, (b * 9) >> 4, jnp.where(b >= 68, b - 12, b))
    late_first = jnp.where(late, jnp.where(b >= 84, b - 72, b - 68), (b * 7) >> 4)

    def early_to(j):
        j = early_first + j
        return early_blk(jnp.where(j >= EARLY, j - EARLY, j))

    def late_to(j):
        j = late_first + j
        return late_blk(jnp.where(j >= LATE, j - LATE, j))

    @pl.when(jnp.logical_not(jnp.logical_and(mine, jnp.logical_not(late))))
    def _():
        c_copy(early_to(0)).start()

    def early_step(j, carry):
        c_copy(early_to(j)).start()
        return carry

    lax.fori_loop(1, EARLY, early_step, 0, unroll=8)
    rx_g[a] = tx_g[a]

    def await_bytes(ref, sem):
        pltpu.make_async_copy(ref, ref, sem).wait()

    await_bytes(rx_g.at[pl.ds(0, 3)], g_recv)
    for k in range(4):
        t_s[32 * k : 32 * k + 32, :] = rx_g[k, 0:32, :].astype(F32)
        w_s[32 * k : 32 * k + 32, :] = rx_g[k, 32:64, :].astype(F32)
    parts = [rx_g[k, 64:80, :].astype(F32) for k in range(4)]
    parts = [parts[0] + parts[1], parts[2] + parts[3]]
    m, n = iota((32, 512), 0), iota((32, 512), 1)
    pick = jnp.logical_and(
        (m >> 4) == ((n & 127) >> 6),
        jnp.logical_and((m & 15) // 3 == (n >> 7), (m & 15) < 12),
    )
    spread = dot(
        jnp.transpose(jnp.concatenate(parts, axis=0)).astype(BF16), ones_where(pick), ((1,), (0,))
    )
    prm[0] = spread[:, 0:128] * (-1.66 * LOG2E)
    prm[1] = spread[:, 128:256] * LOG2E
    prm[2] = spread[:, 256:384]
    prm[3] = spread[:, 384:512]

    power = [prm[1, 8 * i : 8 * i + 8, :] for i in range(16)]

    def absorb(k, sums):
        sums = list(sums)
        rows_t = [jnp.broadcast_to(t_s[pl.ds(4 * k + u, 1), :], (8, 128)) for u in range(4)]
        rows_w = [jnp.broadcast_to(w_s[pl.ds(4 * k + u, 1), :], (8, 128)) for u in range(4)]
        for u in range(4):
            for i in range(16):
                x = rows_w[u] * jnp.exp2(power[i] * rows_t[u])
                xs[4 * k + u, 8 * i : 8 * i + 8, :] = x
                sums[i] = sums[i] + x
        return tuple(sums)

    sums = lax.fori_loop(0, 32, absorb, tuple(jnp.zeros((8, 128), F32) for i in range(16)))

    sums = jnp.transpose(jnp.concatenate(sums, axis=0))
    for k in range(4):
        tx_s[:, k, :] = sums[32 * k : 32 * k + 32]

    @pl.when(mine)
    def _():
        pltpu.make_async_copy(tx_s.at[b_lo], rx_s.at[b_lo], s_recv).start()

    def s_sends(to_late):
        def step(j, carry):
            to = (b_lo + j) & 31
            wanted = is_late(32 * a + to) == to_late

            @pl.when(jnp.logical_and(wanted, jnp.logical_not(jnp.logical_and(mine, j == 0))))
            def _():
                pltpu.make_async_remote_copy(
                    src_ref=tx_s.at[to],
                    dst_ref=rx_s.at[b_lo],
                    send_sem=s_send,
                    recv_sem=s_recv,
                    device_id=(32 * a + to, b_hi),
                    device_id_type=MESH,
                ).start()

            return carry

        lax.fori_loop(0, 32, step, 0)

    @pl.when(a < 3)
    def _():
        s_sends(False)

    @pl.when(core == 0)
    def _():
        pl.semaphore_wait(pair_sem, 1)

    @pl.when(core == 1)
    def _():
        pl.semaphore_wait(bar, LATE + 1 - self_counted)
        pl.semaphore_signal(pair_sem, inc=1, device_id=sibling, device_id_type=MESH)

    @pl.when(jnp.logical_not(jnp.logical_and(mine, late)))
    def _():
        c_copy(late_to(0)).start()

    def late_step(j, carry):
        c_copy(late_to(j)).start()
        return carry

    lax.fori_loop(1, LATE, late_step, 0, unroll=5)

    @pl.when(a >= 2)
    def _():
        s_sends(True)

    m, n = iota((256, 512), 0), iota((256, 512), 1)
    slot = m & 127
    pick = jnp.logical_and((slot >> 5) == (n >> 7), (n & 63) == (m >> 7) * 32 + (slot & 31))
    pick = ones_where(pick)
    await_bytes(rx_c, c_recv)
    got = jnp.transpose(rx_c[:, 0, :])
    both = jnp.concatenate([got[0:32], got[32:64]], axis=1).astype(BF16)
    cond = dot(both, pick, ((1,), (0,)))
    for k in range(4):
        c_s[32 * k : 32 * k + 32, :] = cond[:, 128 * k : 128 * k + 128]
    sun = got[64:72]
    first = sun[0:1] + sun[1:2] + sun[2:3]
    second = jnp.broadcast_to(sun[3:4] + sun[4:5] + sun[5:6], (8, 128))
    lane = iota((8, 128), 1)
    sun = jnp.where((lane & 63) < 32, jnp.broadcast_to(first, (8, 128)), pltpu.roll(second, 32, 1))
    sun = jnp.where(lane < 64, sun, 0.0)
    sun = sun + pltpu.roll(sun, 64, 1)

    def h_copy(to):
        return pltpu.make_async_remote_copy(
            src_ref=tx_h.at[to],
            dst_ref=rx_h.at[a],
            send_sem=h_send,
            recv_sem=h_recv,
            device_id=(b, to),
            device_id_type=MESH,
        )

    def levels(first, trans):
        rows_q = [
            jnp.broadcast_to(1.0 + 0.2 * t_s[pl.ds(first + u, 1), :], (8, 128)) for u in range(UNROLL)
        ]
        rows_c = [jnp.broadcast_to(c_s[pl.ds(first + u, 1), :], (8, 128)) for u in range(UNROLL)]
        totals = [None] * UNROLL
        trans = list(trans)
        for u in range(UNROLL):
            for i in range(16):
                rows = slice(8 * i, 8 * i + 8)
                e = jnp.exp2(prm[0, rows, :] * (xs[first + u, rows, :] + rows_c[u]))
                term = (1.0 - e) * (trans[i] - prm[3, rows, :] * rows_q[u])
                trans[i] = trans[i] * e
                totals[u] = term if i == 0 else totals[u] + term
        for u in range(UNROLL):
            acc[first + u] = totals[u]
        return tuple(trans)

    trans = tuple(prm[2, 8 * i : 8 * i + 8, :] * sun for i in range(16))
    def quarter(part, trans):
        first = pl.multiple_of(32 * part, 32)
        trans = lax.fori_loop(
            0, 32 // UNROLL, lambda k, v: levels(first + UNROLL * k, v), trans
        )
        heat = 0.0625 * jnp.sum(acc[pl.ds(first, 32)], axis=1)
        heat = heat + pltpu.roll(heat, 64, 1)

        @pl.when(a == part)
        def _():
            rx_h[part] = heat

        @pl.when(a != part)
        def _():
            tx_h[part] = heat
            h_copy(part).start()

        return trans

    lax.fori_loop(0, 4, quarter, trans)

    await_bytes(rx_s, s_recv)
    lane, row = iota((32, 128), 1), iota((32, 128), 0)
    c_all = jnp.broadcast_to(
        jnp.sum(parts[0][12:15] + parts[1][12:15], axis=0, keepdims=True), (32, 128)
    )
    mu_all = jnp.broadcast_to(mu_in[...], (32, 256))
    lane2, row2 = iota((32, 256), 1), iota((32, 256), 0)
    rows = None
    for r in range(2):
        at = 2 * row + r
        c_col = jnp.sum(jnp.where(lane == (a & 1) * 64 + at, c_all, 0.0), axis=1, keepdims=True)
        mu_col = jnp.sum(
            jnp.where(lane2 == a * 64 + 2 * row2 + r, mu_all, 0.0), axis=1, keepdims=True
        )
        flux = None
        for half in range(2):
            par = parts[half]
            factor = jnp.sum(par[0:3], axis=0, keepdims=True) * (-1.66 * LOG2E)
            weight = jnp.sum(par[6:9], axis=0, keepdims=True)
            term = weight * jnp.exp2(factor * (rx_s[:, 2 * half + r, :] + c_col))
            flux = term if flux is None else flux + term
        flux = jnp.sum(flux, axis=1, keepdims=True) * jnp.maximum(mu_col, 0.0)
        flux = jnp.where(lane == at, flux, 0.0)
        rows = flux if rows is None else rows + flux
    surf_ref[...] = jnp.sum(rows, axis=0, keepdims=True)[:, 0:64]

    await_bytes(rx_h.at[pl.ds(0, 3)], h_recv)
    heat = jnp.concatenate([rx_h[k] for k in range(4)], axis=1)
    heat = jnp.where((iota((32, 512), 1) & 127) < 64, heat, 0.0)
    heat = dot(jnp.concatenate(split3(heat), axis=0), onehot[...], ((1,), (0,)))
    heat_ref[...] = heat[0:32] + heat[32:64] + heat[64:96]

    await_bytes(tx_g.at[pl.ds(0, 3)], g_send)
    await_bytes(tx_h.at[pl.ds(0, 3)], h_send)

    @pl.when(mine)
    def _():
        await_bytes(tx_c.at[pl.ds(0, 127)], c_send)
        await_bytes(tx_s.at[pl.ds(0, 31)], s_send)

    @pl.when(jnp.logical_not(mine))
    def _():
        await_bytes(tx_c, c_send)
        await_bytes(tx_s, s_send)


def place(heat_in, surf_in, heat_out, surf_out, sem):
    copies = [
        pltpu.make_async_copy(heat_in, heat_out, sem.at[0]),
        pltpu.make_async_copy(surf_in, surf_out, sem.at[1]),
    ]
    for copy in copies:
        copy.start()
    for copy in copies:
        copy.wait()


def shards(
    thermal_deviation, moisture_mass, condensate_optic, sun_height_factor, group_assignment,
    opacity_factor, thermal_power, sunlight_weights, thermal_weights,
):
    vmem = pl.BlockSpec(memory_space=pltpu.VMEM)
    heating, surface = pl.pallas_call(
        kernel,
        out_shape=(
            jax.ShapeDtypeStruct((32, 256), F32),
            jax.ShapeDtypeStruct((1, 64), F32),
        ),
        in_specs=[pl.BlockSpec(memory_space=pltpu.HBM)] * 9,
        out_specs=(vmem, vmem),
        scratch_shapes=[
            pltpu.VMEM((32, 256), BF16),
            pltpu.VMEM((32, 256), BF16),
            pltpu.VMEM((32, 256), BF16),
            pltpu.VMEM((1, 256), F32),
            pltpu.VMEM((1, 256), jnp.int32),
            pltpu.VMEM((1, 64), F32),
            pltpu.VMEM((1, 64), F32),
            pltpu.VMEM((1, 64), F32),
            pltpu.VMEM((1, 64), F32),
            pltpu.VMEM((128, 1, 128), F32),
            pltpu.VMEM((128, 1, 128), F32),
            pltpu.VMEM((4, 80, 128), BF16),
            pltpu.VMEM((4, 80, 128), BF16),
            pltpu.VMEM((4, 32, 128), F32),
            pltpu.VMEM((4, 32, 128), F32),
            pltpu.VMEM((32, 4, 128), F32),
            pltpu.VMEM((32, 4, 128), F32),
            pltpu.VMEM((512, 256), BF16),
            pltpu.VMEM((128, 128), F32),
            pltpu.VMEM((128, 128), F32),
            pltpu.VMEM((128, 128), F32),
            pltpu.VMEM((4, 128, 128), F32),
            pltpu.VMEM((128, 8, 128), F32),
            pltpu.VMEM((128, 128, 128), F32),
            pltpu.SemaphoreType.DMA((9,)),
        ]
        + [pltpu.SemaphoreType.DMA] * 8
        + [pltpu.SemaphoreType.REGULAR],
        compiler_params=pltpu.CompilerParams(
            collective_id=0, has_side_effects=True, vmem_limit_bytes=32 * 1024 * 1024
        ),
    )(
        *(
            pltpu.with_memory_space_constraint(v, pltpu.HBM)
            for v in (
                thermal_deviation.T,
                moisture_mass.T,
                condensate_optic.T,
                sun_height_factor.reshape(1, -1),
                group_assignment.reshape(1, -1),
                opacity_factor.reshape(1, -1),
                thermal_power.reshape(1, -1),
                sunlight_weights.reshape(1, -1),
                thermal_weights.reshape(1, -1),
            )
        )
    )
    heating, surface = pl.pallas_call(
        place,
        out_shape=(
            jax.ShapeDtypeStruct((32, 256), F32),
            jax.ShapeDtypeStruct((1, 64), F32),
        ),
        in_specs=[vmem] * 2,
        out_specs=[pl.BlockSpec(memory_space=pltpu.HBM)] * 2,
        scratch_shapes=[pltpu.SemaphoreType.DMA((2,))],
    )(*(pltpu.with_memory_space_constraint(v, pltpu.VMEM) for v in (heating, surface)))
    return heating.T, surface.reshape(-1)


def solution(mesh):
    in_specs = (
        P("blk", "ga"), P("blk", "ga"), P("blk", "ga"), P("blk"), P("blk"),
        P("ga"), P("ga"), P("ga"), P("ga"),
    )
    out_specs = (P("blk", "ga"), P(("blk", "ga")))
    return jax.shard_map(shards, mesh=mesh, in_specs=in_specs, out_specs=out_specs, check_vma=False)
```

```python
import jax
import jax.numpy as jnp
from jax import lax
from jax.experimental import pallas as pl
from jax.experimental.pallas import tpu as pltpu
from jax.sharding import PartitionSpec as P

F32 = jnp.float32
BF16 = jnp.bfloat16
UNROLL = 8
LOG2E = 1.4426950408889634
MESH = pl.DeviceIdType.MESH


def iota(shape, dim):
    return lax.broadcasted_iota(jnp.int32, shape, dim)


def split3(v):
    hi = v.astype(BF16)
    rest = v - hi.astype(F32)
    mid = rest.astype(BF16)
    lo = (rest - mid.astype(F32)).astype(BF16)
    return hi, mid, lo


def dot(x, y, dims):
    return lax.dot_general(x, y, (dims, ((), ())), preferred_element_type=F32)


def ones_where(cond):
    return jnp.where(cond, 1.0, 0.0).astype(BF16)


EARLY, LATE = 72, 56


def is_late(blk):
    return jnp.logical_or(blk >= 96, jnp.logical_and(blk >= 64, (blk & 15) >= 4))


def kernel(
    t_hbm, w_hbm, c_hbm, mu_hbm, g_hbm, op_hbm, tp_hbm, sw_hbm, tw_hbm,
    heat_ref, surf_ref,
    t_in, w_in, c_in, mu_in, g_in, op_in, tp_in, sw_in, tw_in,
    tx_c, rx_c, tx_g, rx_g, tx_h, rx_h, tx_s, rx_s,
    onehot, t_s, w_s, c_s, c_above, prm, acc, xs, emit, above,
    in_sem, c_send, c_recv, g_send, g_recv, h_send, h_recv, s_send_sem, s_recv, pair_sem,
):
    b = lax.axis_index("blk")
    a = lax.axis_index("ga")
    b_hi, b_lo = b >> 5, b & 31
    mine = b_hi == a
    core = b & 1
    late = is_late(b)
    sibling = (b ^ 1, a)

    loads = [
        pltpu.make_async_copy(src, dst, in_sem.at[i])
        for i, (src, dst) in enumerate(
            (
                (c_hbm, c_in), (mu_hbm, mu_in), (g_hbm, g_in), (t_hbm, t_in), (w_hbm, w_in),
                (op_hbm, op_in), (tp_hbm, tp_in), (sw_hbm, sw_in), (tw_hbm, tw_in),
            )
        )
    ]
    for load in loads:
        load.start()

    bar = pltpu.get_barrier_semaphore()

    def greet(dev):
        pl.semaphore_signal(bar, inc=1, device_id=dev, device_id_type=MESH)

    greet(sibling)
    for k in range(1, 4):
        greet((b & 126, (a + k) & 3))
    told = jnp.where(late, 1, 0)
    told_self = jnp.logical_and(mine, core == told)

    def announce(j):
        greet((32 * a + told + ((2 * (j >> 2)) ^ (b_lo & 30)), (a ^ j) & 3))

    @pl.when(jnp.logical_not(told_self))
    def _():
        announce(0)

    def announce_step(j, carry):
        announce(j)
        return carry

    lax.fori_loop(1, 64, announce_step, 0, unroll=9)

    loads[0].wait()
    loads[1].wait()
    c_t = c_in[...]
    sun_row = jnp.maximum(mu_in[...], 0.0)
    row, col = iota((16, 512), 0), iota((16, 512), 1)
    sun_two = jnp.broadcast_to(jnp.concatenate([sun_row, sun_row], axis=1), (16, 512))
    sun_tile = jnp.zeros((16, 512), F32)
    for s, part in enumerate(split3(sun_two)):
        sun_tile = jnp.where(row == 3 * (col >> 8) + s, part.astype(F32), sun_tile)
    none = jnp.zeros((32, 256), BF16)
    laid = jnp.concatenate(
        [
            jnp.concatenate([c_t, none], axis=1),
            jnp.concatenate([none, c_t], axis=1),
            sun_tile.astype(BF16),
            jnp.zeros((48, 512), BF16),
        ],
        axis=0,
    )
    row, col = iota((128, 512), 0), iota((128, 512), 1)
    pick = ones_where((col & 255) == 2 * row + (col >> 8))
    tx_c[:, 0, :] = dot(pick, laid, ((1,), (1,)))

    loads[2].wait()
    groups = g_in[...]
    member = groups == iota((128, 256), 0)
    earlier = ones_where(iota((256, 256), 0) < iota((256, 256), 1))
    before = dot(ones_where(member), earlier, ((1,), (0,)))
    second = jnp.sum(jnp.where(member, before, 0.0), axis=0, keepdims=True).astype(jnp.int32)
    place = (groups >> 5) * 128 + second * 32 + (groups & 31)
    n = iota((512, 256), 0)
    hot = ones_where((n & 447) == place)
    onehot[...] = hot
    loads[3].wait()
    loads[4].wait()
    moved = dot(jnp.concatenate([t_in[...], w_in[...]], axis=0), hot, ((1,), (1,))).astype(BF16)
    for k in range(4):
        tx_g[k, 0:64, :] = moved[:, 128 * k : 128 * k + 128]

    for load in loads[5:]:
        load.wait()
    row, lane = iota((16, 128), 0), iota((16, 128), 1)
    tile = jnp.zeros((16, 128), F32)
    for j, ref in enumerate((op_in, tp_in, sw_in, tw_in)):
        v = ref[...]
        v = jnp.broadcast_to(jnp.concatenate([v, v], axis=1), (16, 128))
        for s, part in enumerate(split3(v)):
            tile = jnp.where(row == 3 * j + s, part.astype(F32), tile)
    tile = jnp.where((lane >> 6) == (a & 1), tile, 0.0)
    c_sum = jnp.sum(c_t.astype(F32), axis=0, keepdims=True)
    for k in range(2):
        v = jnp.broadcast_to(c_sum[:, 128 * k : 128 * k + 128], (16, 128))
        full = tile
        for s, part in enumerate(split3(v)):
            full = jnp.where(row == 12 + s, part.astype(F32), full)
        for half in range(2):
            tx_g[2 * k + half, 64:80, :] = full.astype(BF16)

    self_counted = jnp.where(told_self, 1, 0)

    @pl.when(core == 0)
    def _():
        pl.semaphore_wait(bar, EARLY + 7 - self_counted)
        pl.semaphore_signal(pair_sem, inc=1, device_id=sibling, device_id_type=MESH)

    @pl.when(core == 1)
    def _():
        pl.semaphore_wait(pair_sem, 1)

    def c_copy(to):
        return pltpu.make_async_remote_copy(
            src_ref=tx_c.at[to],
            dst_ref=rx_c.at[a * 32 + b_lo],
            send_sem=c_send,
            recv_sem=c_recv,
            device_id=(to, b_hi),
            device_id_type=MESH,
        )

    def g_copy(k):
        to = (a + k) & 3
        return pltpu.make_async_remote_copy(
            src_ref=tx_g.at[to],
            dst_ref=rx_g.at[a],
            send_sem=g_send,
            recv_sem=g_recv,
            device_id=(b, to),
            device_id_type=MESH,
        )

    for k in range(1, 4):
        g_copy(k).start()

    @pl.when(mine)
    def _():
        pltpu.make_async_copy(tx_c.at[b], rx_c.at[a * 32 + b_lo], c_recv).start()

    @pl.when(jnp.logical_not(jnp.logical_and(mine, b < 64)))
    def _():
        c_copy(b & 63).start()

    def early_step(j, carry):
        c_copy(j ^ (b & 63)).start()
        return carry

    lax.fori_loop(1, 64, early_step, 0, unroll=9)

    def between(members):
        for j in members:
            to = (64 + j) ^ (b & 19)

            @pl.when(jnp.logical_not(jnp.logical_and(mine, b == to)))
            def _():
                c_copy(to).start()

    between([j for j in range(32) if j & 15 < 4])
    rx_g[a] = tx_g[a]

    def await_bytes(ref, sem):
        pltpu.make_async_copy(ref, ref, sem).wait()

    await_bytes(rx_g.at[pl.ds(0, 3)], g_recv)
    for k in range(4):
        t_s[32 * k : 32 * k + 32, :] = rx_g[k, 0:32, :].astype(F32)
        w_s[32 * k : 32 * k + 32, :] = rx_g[k, 32:64, :].astype(F32)
    parts = [rx_g[k, 64:80, :].astype(F32) for k in range(4)]
    parts = [parts[0] + parts[1], parts[2] + parts[3]]
    m, n = iota((32, 512), 0), iota((32, 512), 1)
    pick = jnp.logical_and(
        (m >> 4) == ((n & 127) >> 6),
        jnp.logical_and((m & 15) // 3 == (n >> 7), (m & 15) < 12),
    )
    spread = dot(
        jnp.transpose(jnp.concatenate(parts, axis=0)).astype(BF16), ones_where(pick), ((1,), (0,))
    )
    prm[0] = spread[:, 0:128] * (-1.66 * LOG2E)
    prm[1] = spread[:, 128:256] * LOG2E
    prm[2] = spread[:, 256:384]
    prm[3] = spread[:, 384:512]

    power = [prm[1, 8 * i : 8 * i + 8, :] for i in range(16)]

    def absorb(k, sums):
        sums = list(sums)
        rows_t = [jnp.broadcast_to(t_s[pl.ds(4 * k + u, 1), :], (8, 128)) for u in range(4)]
        rows_w = [jnp.broadcast_to(w_s[pl.ds(4 * k + u, 1), :], (8, 128)) for u in range(4)]
        for u in range(4):
            for i in range(16):
                x = rows_w[u] * jnp.exp2(power[i] * rows_t[u])
                xs[4 * k + u, 8 * i : 8 * i + 8, :] = x
                sums[i] = sums[i] + x
        return tuple(sums)

    sums = tuple(jnp.zeros((8, 128), F32) for i in range(16))
    for k in range(4):
        for i in range(16):
            above[k, 8 * i : 8 * i + 8, :] = sums[i]
        sums = lax.fori_loop(8 * k, 8 * k + 8, absorb, sums)

    sums = jnp.transpose(jnp.concatenate(sums, axis=0))
    for k in range(4):
        tx_s[:, k, :] = sums[32 * k : 32 * k + 32]

    @pl.when(mine)
    def _():
        pltpu.make_async_copy(tx_s.at[b_lo], rx_s.at[b_lo], s_recv).start()

    def s_send(to):
        pltpu.make_async_remote_copy(
            src_ref=tx_s.at[to],
            dst_ref=rx_s.at[b_lo],
            send_sem=s_send_sem,
            recv_sem=s_recv,
            device_id=(32 * a + to, b_hi),
            device_id_type=MESH,
        ).start()

    def s_sends(to_late):
        @pl.when(a == 2)
        def _():
            def step(to, carry):
                wanted = is_late(64 + to) == to_late

                @pl.when(jnp.logical_and(wanted, jnp.logical_not(jnp.logical_and(mine, to == b_lo))))
                def _():
                    s_send(to)

                return carry

            lax.fori_loop(0, 32, step, 0)

        @pl.when(a == 3 if to_late else a < 2)
        def _():
            @pl.when(jnp.logical_not(mine))
            def _():
                s_send(b_lo)

            def step(j, carry):
                s_send((b_lo + j) & 31)
                return carry

            lax.fori_loop(1, 32, step, 0, unroll=31)

    s_sends(False)

    @pl.when(core == 0)
    def _():
        pl.semaphore_wait(pair_sem, 1)

    @pl.when(core == 1)
    def _():
        pl.semaphore_wait(bar, LATE + 1 - self_counted)
        pl.semaphore_signal(pair_sem, inc=1, device_id=sibling, device_id_type=MESH)

    @pl.when(jnp.logical_not(jnp.logical_and(mine, b >= 96)))
    def _():
        c_copy(96 + b_lo).start()

    def late_step(j, carry):
        c_copy(96 + (j ^ b_lo)).start()
        return carry

    lax.fori_loop(1, 32, late_step, 0, unroll=31)
    between([j for j in range(32) if j & 15 >= 4])

    s_sends(True)

    weight = [prm[3, 8 * i : 8 * i + 8, :] for i in range(16)]

    def radiate(k, carry):
        k = pl.multiple_of(8 * k, 8)
        for u in range(8):
            q = jnp.broadcast_to(1.0 + 0.2 * t_s[pl.ds(k + u, 1), :], (8, 128))
            for i in range(16):
                emit[k + u, 8 * i : 8 * i + 8, :] = weight[i] * q
        return carry

    lax.fori_loop(0, 16, radiate, 0)

    m, n = iota((256, 512), 0), iota((256, 512), 1)
    slot = m & 127
    pick = jnp.logical_and((slot >> 5) == (n >> 7), (n & 63) == (m >> 7) * 32 + (slot & 31))
    pick = ones_where(pick)
    await_bytes(rx_c, c_recv)
    got = jnp.transpose(rx_c[:, 0, :])
    both = jnp.concatenate([got[0:32], got[32:64]], axis=1).astype(BF16)
    cond = dot(both, pick, ((1,), (0,)))
    c_sums = jnp.zeros((1, 128), F32)
    for k in range(4):
        part = cond[:, 128 * k : 128 * k + 128]
        c_s[32 * k : 32 * k + 32, :] = part
        c_above[k] = jnp.broadcast_to(c_sums, (8, 128))
        c_sums = c_sums + jnp.sum(part, axis=0, keepdims=True)
    sun = got[64:72]
    first = sun[0:1] + sun[1:2] + sun[2:3]
    second = jnp.broadcast_to(sun[3:4] + sun[4:5] + sun[5:6], (8, 128))
    lane = iota((8, 128), 1)
    sun = jnp.where((lane & 63) < 32, jnp.broadcast_to(first, (8, 128)), pltpu.roll(second, 32, 1))
    sun = jnp.where(lane < 64, sun, 0.0)
    sun = sun + pltpu.roll(sun, 64, 1)

    def h_copy(to):
        return pltpu.make_async_remote_copy(
            src_ref=tx_h.at[to],
            dst_ref=rx_h.at[a],
            send_sem=h_send,
            recv_sem=h_recv,
            device_id=(b, to),
            device_id_type=MESH,
        )

    def levels(first, trans):
        rows_c = [jnp.broadcast_to(c_s[pl.ds(first + u, 1), :], (8, 128)) for u in range(UNROLL)]
        totals = [None] * UNROLL
        trans = list(trans)
        for u in range(UNROLL):
            for i in range(16):
                rows = slice(8 * i, 8 * i + 8)
                e = jnp.exp2(prm[0, rows, :] * (xs[first + u, rows, :] + rows_c[u]))
                term = (1.0 - e) * (trans[i] - emit[first + u, rows, :])
                trans[i] = trans[i] * e
                totals[u] = term if i == 0 else totals[u] + term
        for u in range(UNROLL):
            acc[first + u] = totals[u]
        return tuple(trans)

    def quarter(step, carry):
        part = (a + jnp.where(step == 0, 2, jnp.where(step == 1, 1, jnp.where(step == 2, 3, 0)))) & 3
        first = pl.multiple_of(32 * part, 32)
        c = c_above[part]
        trans = []
        for i in range(16):
            rows = slice(8 * i, 8 * i + 8)
            depth = prm[0, rows, :] * (above[part, rows, :] + c)
            trans.append(prm[2, rows, :] * sun * jnp.exp2(depth))
        lax.fori_loop(
            0, 32 // UNROLL, lambda k, v: levels(pl.multiple_of(first + UNROLL * k, UNROLL), v), tuple(trans)
        )
        heat = 0.0625 * jnp.sum(acc[pl.ds(first, 32)], axis=1)
        heat = heat + pltpu.roll(heat, 64, 1)

        @pl.when(step == 3)
        def _():
            rx_h[part] = heat

        @pl.when(step < 3)
        def _():
            tx_h[part] = heat
            h_copy(part).start()

        return carry

    lax.fori_loop(0, 4, quarter, 0)

    await_bytes(rx_s, s_recv)
    lane, row = iota((32, 128), 1), iota((32, 128), 0)
    c_all = jnp.broadcast_to(
        jnp.sum(parts[0][12:15] + parts[1][12:15], axis=0, keepdims=True), (32, 128)
    )
    mu_all = jnp.broadcast_to(mu_in[...], (32, 256))
    lane2, row2 = iota((32, 256), 1), iota((32, 256), 0)
    rows = None
    for r in range(2):
        at = 2 * row + r
        c_col = jnp.sum(jnp.where(lane == (a & 1) * 64 + at, c_all, 0.0), axis=1, keepdims=True)
        mu_col = jnp.sum(
            jnp.where(lane2 == a * 64 + 2 * row2 + r, mu_all, 0.0), axis=1, keepdims=True
        )
        flux = None
        for half in range(2):
            par = parts[half]
            factor = jnp.sum(par[0:3], axis=0, keepdims=True) * (-1.66 * LOG2E)
            weight = jnp.sum(par[6:9], axis=0, keepdims=True)
            term = weight * jnp.exp2(factor * (rx_s[:, 2 * half + r, :] + c_col))
            flux = term if flux is None else flux + term
        flux = jnp.sum(flux, axis=1, keepdims=True) * jnp.maximum(mu_col, 0.0)
        flux = jnp.where(lane == at, flux, 0.0)
        rows = flux if rows is None else rows + flux
    surf_ref[...] = jnp.sum(rows, axis=0, keepdims=True)[:, 0:64]

    await_bytes(rx_h.at[pl.ds(0, 3)], h_recv)
    heat = jnp.concatenate([rx_h[k] for k in range(4)], axis=1)
    heat = jnp.where((iota((32, 512), 1) & 127) < 64, heat, 0.0)
    heat = dot(jnp.concatenate(split3(heat), axis=0), onehot[...], ((1,), (0,)))
    heat_ref[...] = heat[0:32] + heat[32:64] + heat[64:96]

    await_bytes(tx_g.at[pl.ds(0, 3)], g_send)
    await_bytes(tx_h.at[pl.ds(0, 3)], h_send)

    @pl.when(mine)
    def _():
        await_bytes(tx_c.at[pl.ds(0, 127)], c_send)
        await_bytes(tx_s.at[pl.ds(0, 31)], s_send_sem)

    @pl.when(jnp.logical_not(mine))
    def _():
        await_bytes(tx_c, c_send)
        await_bytes(tx_s, s_send_sem)


def place(heat_in, surf_in, heat_out, surf_out, sem):
    copies = [
        pltpu.make_async_copy(heat_in, heat_out, sem.at[0]),
        pltpu.make_async_copy(surf_in, surf_out, sem.at[1]),
    ]
    for copy in copies:
        copy.start()
    for copy in copies:
        copy.wait()


def shards(
    thermal_deviation, moisture_mass, condensate_optic, sun_height_factor, group_assignment,
    opacity_factor, thermal_power, sunlight_weights, thermal_weights,
):
    vmem = pl.BlockSpec(memory_space=pltpu.VMEM)
    heating, surface = pl.pallas_call(
        kernel,
        out_shape=(
            jax.ShapeDtypeStruct((32, 256), F32),
            jax.ShapeDtypeStruct((1, 64), F32),
        ),
        in_specs=[pl.BlockSpec(memory_space=pltpu.HBM)] * 9,
        out_specs=(vmem, vmem),
        scratch_shapes=[
            pltpu.VMEM((32, 256), BF16),
            pltpu.VMEM((32, 256), BF16),
            pltpu.VMEM((32, 256), BF16),
            pltpu.VMEM((1, 256), F32),
            pltpu.VMEM((1, 256), jnp.int32),
            pltpu.VMEM((1, 64), F32),
            pltpu.VMEM((1, 64), F32),
            pltpu.VMEM((1, 64), F32),
            pltpu.VMEM((1, 64), F32),
            pltpu.VMEM((128, 1, 128), F32),
            pltpu.VMEM((128, 1, 128), F32),
            pltpu.VMEM((4, 80, 128), BF16),
            pltpu.VMEM((4, 80, 128), BF16),
            pltpu.VMEM((4, 32, 128), F32),
            pltpu.VMEM((4, 32, 128), F32),
            pltpu.VMEM((32, 4, 128), F32),
            pltpu.VMEM((32, 4, 128), F32),
            pltpu.VMEM((512, 256), BF16),
            pltpu.VMEM((128, 128), F32),
            pltpu.VMEM((128, 128), F32),
            pltpu.VMEM((128, 128), F32),
            pltpu.VMEM((4, 8, 128), F32),
            pltpu.VMEM((4, 128, 128), F32),
            pltpu.VMEM((128, 8, 128), F32),
            pltpu.VMEM((128, 128, 128), F32),
            pltpu.VMEM((128, 128, 128), F32),
            pltpu.VMEM((4, 128, 128), F32),
            pltpu.SemaphoreType.DMA((9,)),
        ]
        + [pltpu.SemaphoreType.DMA] * 8
        + [pltpu.SemaphoreType.REGULAR],
        compiler_params=pltpu.CompilerParams(
            collective_id=0, has_side_effects=True, vmem_limit_bytes=32 * 1024 * 1024
        ),
    )(
        *(
            pltpu.with_memory_space_constraint(v, pltpu.HBM)
            for v in (
                thermal_deviation.T,
                moisture_mass.T,
                condensate_optic.T,
                sun_height_factor.reshape(1, -1),
                group_assignment.reshape(1, -1),
                opacity_factor.reshape(1, -1),
                thermal_power.reshape(1, -1),
                sunlight_weights.reshape(1, -1),
                thermal_weights.reshape(1, -1),
            )
        )
    )
    heating, surface = pl.pallas_call(
        place,
        out_shape=(
            jax.ShapeDtypeStruct((32, 256), F32),
            jax.ShapeDtypeStruct((1, 64), F32),
        ),
        in_specs=[vmem] * 2,
        out_specs=[pl.BlockSpec(memory_space=pltpu.HBM)] * 2,
        scratch_shapes=[pltpu.SemaphoreType.DMA((2,))],
    )(*(pltpu.with_memory_space_constraint(v, pltpu.VMEM) for v in (heating, surface)))
    return heating.T, surface.reshape(-1)


def solution(mesh):
    in_specs = (
        P("blk", "ga"), P("blk", "ga"), P("blk", "ga"), P("blk"), P("blk"),
        P("ga"), P("ga"), P("ga"), P("ga"),
    )
    out_specs = (P("blk", "ga"), P(("blk", "ga")))
    return jax.shard_map(shards, mesh=mesh, in_specs=in_specs, out_specs=out_specs, check_vma=False)
```

```python
import jax
import jax.numpy as jnp
from jax import lax
from jax.experimental import pallas as pl
from jax.experimental.pallas import tpu as pltpu
from jax.sharding import PartitionSpec as P

F32 = jnp.float32
BF16 = jnp.bfloat16
UNROLL = 8
LOG2E = 1.4426950408889634
MESH = pl.DeviceIdType.MESH


def iota(shape, dim):
    return lax.broadcasted_iota(jnp.int32, shape, dim)


def split3(v):
    hi = v.astype(BF16)
    rest = v - hi.astype(F32)
    mid = rest.astype(BF16)
    lo = (rest - mid.astype(F32)).astype(BF16)
    return hi, mid, lo


def dot(x, y, dims):
    return lax.dot_general(x, y, (dims, ((), ())), preferred_element_type=F32)


def ones_where(cond):
    return jnp.where(cond, 1.0, 0.0).astype(BF16)


EARLY, LATE = 72, 56


def is_late(blk):
    return jnp.logical_or(blk >= 96, jnp.logical_and(blk >= 64, (blk & 15) >= 4))


def kernel(
    t_hbm, w_hbm, c_hbm, mu_hbm, g_hbm, op_hbm, tp_hbm, sw_hbm, tw_hbm,
    heat_ref, surf_ref,
    t_in, w_in, c_in, mu_in, g_in, op_in, tp_in, sw_in, tw_in,
    tx_c, rx_c, tx_g, rx_g, tx_h, rx_h, tx_s, rx_s,
    onehot, t_s, w_s, c_s, c_above, prm, acc, xs, emit, above,
    in_sem, c_send, c_recv, g_send, g_recv, h_send, h_recv, s_send_sem, s_recv, line_sem, early_sem, late_sem,
):
    b = lax.axis_index("blk")
    a = lax.axis_index("ga")
    b_hi, b_lo = b >> 5, b & 31
    mine = b_hi == a
    core = b & 1
    late = is_late(b)
    sibling = (b ^ 1, a)
    line = [(b, a ^ k) for k in range(1, 4)] + [(b ^ 1, a ^ k) for k in range(4)]
    counts_early = jnp.logical_and(core == 0, mine)
    counts_late = jnp.logical_and(core == 1, (a ^ 1) == b_hi)
    counts = jnp.logical_or(counts_early, counts_late)

    loads = [
        pltpu.make_async_copy(src, dst, in_sem.at[i])
        for i, (src, dst) in enumerate(
            (
                (c_hbm, c_in), (mu_hbm, mu_in), (g_hbm, g_in), (t_hbm, t_in), (w_hbm, w_in),
                (op_hbm, op_in), (tp_hbm, tp_in), (sw_hbm, sw_in), (tw_hbm, tw_in),
            )
        )
    ]
    for load in loads:
        load.start()

    bar = pltpu.get_barrier_semaphore()

    def greet(dev):
        pl.semaphore_signal(bar, inc=1, device_id=dev, device_id_type=MESH)

    for dev in line:
        greet(dev)
    self_counted = jnp.logical_and(counts_early, jnp.logical_not(late))
    told = jnp.where(late, a ^ 1, a)

    def announce(m):
        greet((32 * a + ((2 * m) ^ (b_lo & 30)) + jnp.where(late, 1, 0), told))

    for m in (4, 12, 5, 13, 3, 11, 6, 14, 2, 10, 7, 15, 1, 9, 8):
        announce(m)

    @pl.when(jnp.logical_not(self_counted))
    def _():
        announce(0)

    loads[0].wait()
    loads[1].wait()
    c_t = c_in[...]
    sun_row = jnp.maximum(mu_in[...], 0.0)
    row, col = iota((16, 512), 0), iota((16, 512), 1)
    sun_two = jnp.broadcast_to(jnp.concatenate([sun_row, sun_row], axis=1), (16, 512))
    sun_tile = jnp.zeros((16, 512), F32)
    for s, part in enumerate(split3(sun_two)):
        sun_tile = jnp.where(row == 3 * (col >> 8) + s, part.astype(F32), sun_tile)
    none = jnp.zeros((32, 256), BF16)
    laid = jnp.concatenate(
        [
            jnp.concatenate([c_t, none], axis=1),
            jnp.concatenate([none, c_t], axis=1),
            sun_tile.astype(BF16),
            jnp.zeros((48, 512), BF16),
        ],
        axis=0,
    )
    row, col = iota((128, 512), 0), iota((128, 512), 1)
    pick = ones_where((col & 255) == 2 * row + (col >> 8))
    tx_c[:, 0, :] = dot(pick, laid, ((1,), (1,)))

    loads[2].wait()
    groups = g_in[...]
    member = groups == iota((128, 256), 0)
    earlier = ones_where(iota((256, 256), 0) < iota((256, 256), 1))
    before = dot(ones_where(member), earlier, ((1,), (0,)))
    second = jnp.sum(jnp.where(member, before, 0.0), axis=0, keepdims=True).astype(jnp.int32)
    place = (groups >> 5) * 128 + second * 32 + (groups & 31)
    n = iota((512, 256), 0)
    hot = ones_where((n & 447) == place)
    onehot[...] = hot
    loads[3].wait()
    loads[4].wait()
    moved = dot(jnp.concatenate([t_in[...], w_in[...]], axis=0), hot, ((1,), (1,))).astype(BF16)
    for k in range(4):
        tx_g[k, 0:64, :] = moved[:, 128 * k : 128 * k + 128]

    for load in loads[5:]:
        load.wait()
    row, lane = iota((16, 128), 0), iota((16, 128), 1)
    tile = jnp.zeros((16, 128), F32)
    for j, ref in enumerate((op_in, tp_in, sw_in, tw_in)):
        v = ref[...]
        v = jnp.broadcast_to(jnp.concatenate([v, v], axis=1), (16, 128))
        for s, part in enumerate(split3(v)):
            tile = jnp.where(row == 3 * j + s, part.astype(F32), tile)
    tile = jnp.where((lane >> 6) == (a & 1), tile, 0.0)
    c_sum = jnp.sum(c_t.astype(F32), axis=0, keepdims=True)
    for k in range(2):
        v = jnp.broadcast_to(c_sum[:, 128 * k : 128 * k + 128], (16, 128))
        full = tile
        for s, part in enumerate(split3(v)):
            full = jnp.where(row == 12 + s, part.astype(F32), full)
        for half in range(2):
            tx_g[2 * k + half, 64:80, :] = full.astype(BF16)

    def tell(sem, devices):
        for dev in devices:
            pl.semaphore_signal(sem, inc=1, device_id=dev, device_id_type=MESH)

    @pl.when(counts)
    def _():
        pl.semaphore_wait(line_sem, 1)

    @pl.when(jnp.logical_not(counts))
    def _():
        pl.semaphore_wait(bar, 7)

    @pl.when(jnp.logical_or(jnp.logical_and(core == 1, mine), jnp.logical_and(core == 0, (a ^ 1) == b_hi)))
    def _():
        tell(line_sem, [sibling])

    def c_copy(to):
        return pltpu.make_async_remote_copy(
            src_ref=tx_c.at[to],
            dst_ref=rx_c.at[a * 32 + b_lo],
            send_sem=c_send,
            recv_sem=c_recv,
            device_id=(to, b_hi),
            device_id_type=MESH,
        )

    def g_copy(k):
        to = (a + k) & 3
        return pltpu.make_async_remote_copy(
            src_ref=tx_g.at[to],
            dst_ref=rx_g.at[a],
            send_sem=g_send,
            recv_sem=g_recv,
            device_id=(b, to),
            device_id_type=MESH,
        )

    for k in range(1, 4):
        g_copy(k).start()

    @pl.when(counts_early)
    def _():
        pl.semaphore_wait(bar, EARLY + 7 - jnp.where(self_counted, 1, 0))
        tell(early_sem, line)

    @pl.when(jnp.logical_not(counts_early))
    def _():
        pl.semaphore_wait(early_sem, 1)

    @pl.when(mine)
    def _():
        pltpu.make_async_copy(tx_c.at[b], rx_c.at[a * 32 + b_lo], c_recv).start()

    def early_step(j, carry):
        c_copy(j ^ 40 ^ (b & 63)).start()
        return carry

    lax.fori_loop(0, 40, early_step, 0, unroll=8)

    @pl.when(jnp.logical_not(jnp.logical_and(mine, b < 64)))
    def _():
        c_copy(b & 63).start()

    lax.fori_loop(41, 64, early_step, 0, unroll=23)

    def between(members):
        for j in members:
            to = (64 + j) ^ (b & 19)

            @pl.when(jnp.logical_not(jnp.logical_and(mine, b == to)))
            def _():
                c_copy(to).start()

    between([j for j in range(32) if j & 15 < 4])
    rx_g[a] = tx_g[a]

    def await_bytes(ref, sem):
        pltpu.make_async_copy(ref, ref, sem).wait()

    await_bytes(rx_g.at[pl.ds(0, 3)], g_recv)
    for k in range(4):
        t_s[32 * k : 32 * k + 32, :] = rx_g[k, 0:32, :].astype(F32)
        w_s[32 * k : 32 * k + 32, :] = rx_g[k, 32:64, :].astype(F32)
    parts = [rx_g[k, 64:80, :].astype(F32) for k in range(4)]
    parts = [parts[0] + parts[1], parts[2] + parts[3]]
    m, n = iota((32, 512), 0), iota((32, 512), 1)
    pick = jnp.logical_and(
        (m >> 4) == ((n & 127) >> 6),
        jnp.logical_and((m & 15) // 3 == (n >> 7), (m & 15) < 12),
    )
    spread = dot(
        jnp.transpose(jnp.concatenate(parts, axis=0)).astype(BF16), ones_where(pick), ((1,), (0,))
    )
    prm[0] = spread[:, 0:128] * (-1.66 * LOG2E)
    prm[1] = spread[:, 128:256] * LOG2E
    prm[2] = spread[:, 256:384]
    prm[3] = spread[:, 384:512]

    power = [prm[1, 8 * i : 8 * i + 8, :] for i in range(16)]

    def absorb(k, sums):
        sums = list(sums)
        rows_t = [jnp.broadcast_to(t_s[pl.ds(4 * k + u, 1), :], (8, 128)) for u in range(4)]
        rows_w = [jnp.broadcast_to(w_s[pl.ds(4 * k + u, 1), :], (8, 128)) for u in range(4)]
        for u in range(4):
            for i in range(16):
                x = rows_w[u] * jnp.exp2(power[i] * rows_t[u])
                xs[4 * k + u, 8 * i : 8 * i + 8, :] = x
                sums[i] = sums[i] + x
        return tuple(sums)

    sums = tuple(jnp.zeros((8, 128), F32) for i in range(16))
    for k in range(4):
        for i in range(16):
            above[k, 8 * i : 8 * i + 8, :] = sums[i]
        sums = lax.fori_loop(8 * k, 8 * k + 8, absorb, sums)

    sums = jnp.transpose(jnp.concatenate(sums, axis=0))
    for k in range(4):
        tx_s[:, k, :] = sums[32 * k : 32 * k + 32]

    @pl.when(mine)
    def _():
        pltpu.make_async_copy(tx_s.at[b_lo], rx_s.at[b_lo], s_recv).start()

    def s_send(to):
        pltpu.make_async_remote_copy(
            src_ref=tx_s.at[to],
            dst_ref=rx_s.at[b_lo],
            send_sem=s_send_sem,
            recv_sem=s_recv,
            device_id=(32 * a + to, b_hi),
            device_id_type=MESH,
        ).start()

    def s_sends(to_late):
        @pl.when(a == 2)
        def _():
            def step(to, carry):
                wanted = is_late(64 + to) == to_late

                @pl.when(jnp.logical_and(wanted, jnp.logical_not(jnp.logical_and(mine, to == b_lo))))
                def _():
                    s_send(to)

                return carry

            lax.fori_loop(0, 32, step, 0)

        @pl.when(a == 3 if to_late else a < 2)
        def _():
            @pl.when(jnp.logical_not(mine))
            def _():
                s_send(b_lo)

            def step(j, carry):
                s_send((b_lo + j) & 31)
                return carry

            lax.fori_loop(1, 32, step, 0, unroll=31)

    s_sends(False)

    @pl.when(counts_late)
    def _():
        pl.semaphore_wait(bar, LATE + 7)
        tell(late_sem, line)

    @pl.when(jnp.logical_not(counts_late))
    def _():
        pl.semaphore_wait(late_sem, 1)

    def late_step(j, carry):
        c_copy(96 + (j ^ 8 ^ b_lo)).start()
        return carry

    lax.fori_loop(0, 8, late_step, 0, unroll=8)

    @pl.when(jnp.logical_not(jnp.logical_and(mine, b >= 96)))
    def _():
        c_copy(96 + b_lo).start()

    lax.fori_loop(9, 32, late_step, 0, unroll=23)
    between([j for j in range(32) if j & 15 >= 4])

    s_sends(True)

    weight = [prm[3, 8 * i : 8 * i + 8, :] for i in range(16)]

    def radiate(k, carry):
        k = pl.multiple_of(8 * k, 8)
        for u in range(8):
            q = jnp.broadcast_to(1.0 + 0.2 * t_s[pl.ds(k + u, 1), :], (8, 128))
            for i in range(16):
                emit[k + u, 8 * i : 8 * i + 8, :] = weight[i] * q
        return carry

    lax.fori_loop(0, 16, radiate, 0)

    m, n = iota((256, 512), 0), iota((256, 512), 1)
    slot = m & 127
    pick = jnp.logical_and((slot >> 5) == (n >> 7), (n & 63) == (m >> 7) * 32 + (slot & 31))
    pick = ones_where(pick)
    await_bytes(rx_c, c_recv)
    got = jnp.transpose(rx_c[:, 0, :])
    both = jnp.concatenate([got[0:32], got[32:64]], axis=1).astype(BF16)
    cond = dot(both, pick, ((1,), (0,)))
    c_sums = jnp.zeros((1, 128), F32)
    for k in range(4):
        part = cond[:, 128 * k : 128 * k + 128]
        c_s[32 * k : 32 * k + 32, :] = part
        c_above[k] = jnp.broadcast_to(c_sums, (8, 128))
        c_sums = c_sums + jnp.sum(part, axis=0, keepdims=True)
    sun = got[64:72]
    first = sun[0:1] + sun[1:2] + sun[2:3]
    second = jnp.broadcast_to(sun[3:4] + sun[4:5] + sun[5:6], (8, 128))
    lane = iota((8, 128), 1)
    sun = jnp.where((lane & 63) < 32, jnp.broadcast_to(first, (8, 128)), pltpu.roll(second, 32, 1))
    sun = jnp.where(lane < 64, sun, 0.0)
    sun = sun + pltpu.roll(sun, 64, 1)

    def h_copy(to):
        return pltpu.make_async_remote_copy(
            src_ref=tx_h.at[to],
            dst_ref=rx_h.at[a],
            send_sem=h_send,
            recv_sem=h_recv,
            device_id=(b, to),
            device_id_type=MESH,
        )

    def levels(first, trans):
        rows_c = [jnp.broadcast_to(c_s[pl.ds(first + u, 1), :], (8, 128)) for u in range(UNROLL)]
        totals = [None] * UNROLL
        trans = list(trans)
        for u in range(UNROLL):
            for i in range(16):
                rows = slice(8 * i, 8 * i + 8)
                e = jnp.exp2(prm[0, rows, :] * (xs[first + u, rows, :] + rows_c[u]))
                term = (1.0 - e) * (trans[i] - emit[first + u, rows, :])
                trans[i] = trans[i] * e
                totals[u] = term if i == 0 else totals[u] + term
        for u in range(UNROLL):
            acc[first + u] = totals[u]
        return tuple(trans)

    def quarter(step, carry):
        part = (a + jnp.where(step == 0, 2, jnp.where(step == 1, 1, jnp.where(step == 2, 3, 0)))) & 3
        first = pl.multiple_of(32 * part, 32)
        c = c_above[part]
        trans = []
        for i in range(16):
            rows = slice(8 * i, 8 * i + 8)
            depth = prm[0, rows, :] * (above[part, rows, :] + c)
            trans.append(prm[2, rows, :] * sun * jnp.exp2(depth))
        lax.fori_loop(
            0, 32 // UNROLL, lambda k, v: levels(pl.multiple_of(first + UNROLL * k, UNROLL), v), tuple(trans)
        )
        heat = 0.0625 * jnp.sum(acc[pl.ds(first, 32)], axis=1)
        heat = heat + pltpu.roll(heat, 64, 1)

        @pl.when(step == 3)
        def _():
            rx_h[part] = heat

        @pl.when(step < 3)
        def _():
            tx_h[part] = heat
            h_copy(part).start()

        return carry

    lax.fori_loop(0, 4, quarter, 0)

    await_bytes(rx_s, s_recv)
    lane, row = iota((32, 128), 1), iota((32, 128), 0)
    c_all = jnp.broadcast_to(
        jnp.sum(parts[0][12:15] + parts[1][12:15], axis=0, keepdims=True), (32, 128)
    )
    mu_all = jnp.broadcast_to(mu_in[...], (32, 256))
    lane2, row2 = iota((32, 256), 1), iota((32, 256), 0)
    rows = None
    for r in range(2):
        at = 2 * row + r
        c_col = jnp.sum(jnp.where(lane == (a & 1) * 64 + at, c_all, 0.0), axis=1, keepdims=True)
        mu_col = jnp.sum(
            jnp.where(lane2 == a * 64 + 2 * row2 + r, mu_all, 0.0), axis=1, keepdims=True
        )
        flux = None
        for half in range(2):
            par = parts[half]
            factor = jnp.sum(par[0:3], axis=0, keepdims=True) * (-1.66 * LOG2E)
            weight = jnp.sum(par[6:9], axis=0, keepdims=True)
            term = weight * jnp.exp2(factor * (rx_s[:, 2 * half + r, :] + c_col))
            flux = term if flux is None else flux + term
        flux = jnp.sum(flux, axis=1, keepdims=True) * jnp.maximum(mu_col, 0.0)
        flux = jnp.where(lane == at, flux, 0.0)
        rows = flux if rows is None else rows + flux
    surf_ref[...] = jnp.sum(rows, axis=0, keepdims=True)[:, 0:64]

    await_bytes(rx_h.at[pl.ds(0, 3)], h_recv)
    heat = jnp.concatenate([rx_h[k] for k in range(4)], axis=1)
    heat = jnp.where((iota((32, 512), 1) & 127) < 64, heat, 0.0)
    heat = dot(jnp.concatenate(split3(heat), axis=0), onehot[...], ((1,), (0,)))
    heat_ref[...] = heat[0:32] + heat[32:64] + heat[64:96]

    await_bytes(tx_g.at[pl.ds(0, 3)], g_send)
    await_bytes(tx_h.at[pl.ds(0, 3)], h_send)

    @pl.when(mine)
    def _():
        await_bytes(tx_c.at[pl.ds(0, 127)], c_send)
        await_bytes(tx_s.at[pl.ds(0, 31)], s_send_sem)

    @pl.when(jnp.logical_not(mine))
    def _():
        await_bytes(tx_c, c_send)
        await_bytes(tx_s, s_send_sem)


def place(heat_in, surf_in, heat_out, surf_out, sem):
    copies = [
        pltpu.make_async_copy(heat_in, heat_out, sem.at[0]),
        pltpu.make_async_copy(surf_in, surf_out, sem.at[1]),
    ]
    for copy in copies:
        copy.start()
    for copy in copies:
        copy.wait()


def shards(
    thermal_deviation, moisture_mass, condensate_optic, sun_height_factor, group_assignment,
    opacity_factor, thermal_power, sunlight_weights, thermal_weights,
):
    vmem = pl.BlockSpec(memory_space=pltpu.VMEM)
    heating, surface = pl.pallas_call(
        kernel,
        out_shape=(
            jax.ShapeDtypeStruct((32, 256), F32),
            jax.ShapeDtypeStruct((1, 64), F32),
        ),
        in_specs=[pl.BlockSpec(memory_space=pltpu.HBM)] * 9,
        out_specs=(vmem, vmem),
        scratch_shapes=[
            pltpu.VMEM((32, 256), BF16),
            pltpu.VMEM((32, 256), BF16),
            pltpu.VMEM((32, 256), BF16),
            pltpu.VMEM((1, 256), F32),
            pltpu.VMEM((1, 256), jnp.int32),
            pltpu.VMEM((1, 64), F32),
            pltpu.VMEM((1, 64), F32),
            pltpu.VMEM((1, 64), F32),
            pltpu.VMEM((1, 64), F32),
            pltpu.VMEM((128, 1, 128), F32),
            pltpu.VMEM((128, 1, 128), F32),
            pltpu.VMEM((4, 80, 128), BF16),
            pltpu.VMEM((4, 80, 128), BF16),
            pltpu.VMEM((4, 32, 128), F32),
            pltpu.VMEM((4, 32, 128), F32),
            pltpu.VMEM((32, 4, 128), F32),
            pltpu.VMEM((32, 4, 128), F32),
            pltpu.VMEM((512, 256), BF16),
            pltpu.VMEM((128, 128), F32),
            pltpu.VMEM((128, 128), F32),
            pltpu.VMEM((128, 128), F32),
            pltpu.VMEM((4, 8, 128), F32),
            pltpu.VMEM((4, 128, 128), F32),
            pltpu.VMEM((128, 8, 128), F32),
            pltpu.VMEM((128, 128, 128), F32),
            pltpu.VMEM((128, 128, 128), F32),
            pltpu.VMEM((4, 128, 128), F32),
            pltpu.SemaphoreType.DMA((9,)),
        ]
        + [pltpu.SemaphoreType.DMA] * 8
        + [pltpu.SemaphoreType.REGULAR] * 3,
        compiler_params=pltpu.CompilerParams(
            collective_id=0, has_side_effects=True, vmem_limit_bytes=32 * 1024 * 1024
        ),
    )(
        *(
            pltpu.with_memory_space_constraint(v, pltpu.HBM)
            for v in (
                thermal_deviation.T,
                moisture_mass.T,
                condensate_optic.T,
                sun_height_factor.reshape(1, -1),
                group_assignment.reshape(1, -1),
                opacity_factor.reshape(1, -1),
                thermal_power.reshape(1, -1),
                sunlight_weights.reshape(1, -1),
                thermal_weights.reshape(1, -1),
            )
        )
    )
    heating, surface = pl.pallas_call(
        place,
        out_shape=(
            jax.ShapeDtypeStruct((32, 256), F32),
            jax.ShapeDtypeStruct((1, 64), F32),
        ),
        in_specs=[vmem] * 2,
        out_specs=[pl.BlockSpec(memory_space=pltpu.HBM)] * 2,
        scratch_shapes=[pltpu.SemaphoreType.DMA((2,))],
    )(*(pltpu.with_memory_space_constraint(v, pltpu.VMEM) for v in (heating, surface)))
    return heating.T, surface.reshape(-1)


def solution(mesh):
    in_specs = (
        P("blk", "ga"), P("blk", "ga"), P("blk", "ga"), P("blk"), P("blk"),
        P("ga"), P("ga"), P("ga"), P("ga"),
    )
    out_specs = (P("blk", "ga"), P(("blk", "ga")))
    return jax.shard_map(shards, mesh=mesh, in_specs=in_specs, out_specs=out_specs, check_vma=False)
```

```python
import jax
import jax.numpy as jnp
from jax import lax
from jax.experimental import pallas as pl
from jax.experimental.pallas import tpu as pltpu
from jax.sharding import PartitionSpec as P

F32 = jnp.float32
BF16 = jnp.bfloat16
UNROLL = 8
LOG2E = 1.4426950408889634
MESH = pl.DeviceIdType.MESH


def iota(shape, dim):
    return lax.broadcasted_iota(jnp.int32, shape, dim)


def split3(v):
    hi = v.astype(BF16)
    rest = v - hi.astype(F32)
    mid = rest.astype(BF16)
    lo = (rest - mid.astype(F32)).astype(BF16)
    return hi, mid, lo


def dot(x, y, dims):
    return lax.dot_general(x, y, (dims, ((), ())), preferred_element_type=F32)


def ones_where(cond):
    return jnp.where(cond, 1.0, 0.0).astype(BF16)


EARLY, LATE = 72, 56


def is_late(blk):
    return jnp.logical_or(blk >= 96, jnp.logical_and(blk >= 64, (blk & 15) >= 4))


def kernel(
    t_hbm, w_hbm, c_hbm, mu_hbm, g_hbm, op_hbm, tp_hbm, sw_hbm, tw_hbm,
    heat_ref, surf_ref,
    t_in, w_in, c_in, mu_in, g_in, op_in, tp_in, sw_in, tw_in,
    tx_c, rx_c, tx_g, rx_g, tx_h, rx_h, tx_s, rx_s,
    onehot, t_s, w_s, c_s, c_above, prm, acc, xs, emit, above,
    in_sem, c_send, c_recv, g_send, g_recv, h_send, h_recv, s_send_sem, s_recv, line_sem, early_sem, late_sem,
):
    b = lax.axis_index("blk")
    a = lax.axis_index("ga")
    b_hi, b_lo = b >> 5, b & 31
    mine = b_hi == a
    core = b & 1
    late = is_late(b)
    sibling = (b ^ 1, a)
    line = [(b, a ^ k) for k in range(1, 4)] + [(b ^ 1, a ^ k) for k in range(4)]
    counts_early = jnp.logical_and(core == 0, mine)
    counts_late = jnp.logical_and(core == 1, (a ^ 1) == b_hi)
    counts = jnp.logical_or(counts_early, counts_late)

    loads = [
        pltpu.make_async_copy(src, dst, in_sem.at[i])
        for i, (src, dst) in enumerate(
            (
                (c_hbm, c_in), (mu_hbm, mu_in), (g_hbm, g_in), (t_hbm, t_in), (w_hbm, w_in),
                (op_hbm, op_in), (tp_hbm, tp_in), (sw_hbm, sw_in), (tw_hbm, tw_in),
            )
        )
    ]
    for load in loads:
        load.start()

    bar = pltpu.get_barrier_semaphore()

    def greet(dev):
        pl.semaphore_signal(bar, inc=1, device_id=dev, device_id_type=MESH)

    for dev in line:
        greet(dev)
    self_counted = jnp.logical_and(counts_early, jnp.logical_not(late))
    told = jnp.where(late, a ^ 1, a)

    def announce(m):
        greet((32 * a + ((2 * m) ^ (b_lo & 30)) + jnp.where(late, 1, 0), told))

    for m in (4, 12, 5, 13, 3, 11, 6, 14, 2, 10, 7, 15, 1, 9, 8):
        announce(m)

    @pl.when(jnp.logical_not(self_counted))
    def _():
        announce(0)

    loads[0].wait()
    loads[1].wait()
    c_t = c_in[...]
    sun_row = jnp.maximum(mu_in[...], 0.0)
    row, col = iota((16, 512), 0), iota((16, 512), 1)
    sun_two = jnp.broadcast_to(jnp.concatenate([sun_row, sun_row], axis=1), (16, 512))
    sun_tile = jnp.zeros((16, 512), F32)
    for s, part in enumerate(split3(sun_two)):
        sun_tile = jnp.where(row == 3 * (col >> 8) + s, part.astype(F32), sun_tile)
    none = jnp.zeros((32, 256), BF16)
    laid = jnp.concatenate(
        [
            jnp.concatenate([c_t, none], axis=1),
            jnp.concatenate([none, c_t], axis=1),
            sun_tile.astype(BF16),
            jnp.zeros((48, 512), BF16),
        ],
        axis=0,
    )
    row, col = iota((128, 512), 0), iota((128, 512), 1)
    pick = ones_where((col & 255) == 2 * row + (col >> 8))
    tx_c[:, 0, :] = dot(pick, laid, ((1,), (1,)))

    def tell(sem, devices):
        for dev in devices:
            pl.semaphore_signal(sem, inc=1, device_id=dev, device_id_type=MESH)

    def count_early():
        pl.semaphore_wait(bar, EARLY + 7 - jnp.where(self_counted, 1, 0))
        tell(early_sem, line)

    @pl.when(jnp.logical_and(counts_early, b_hi >= 2))
    def _():
        count_early()

    loads[2].wait()
    groups = g_in[...]
    member = groups == iota((128, 256), 0)
    earlier = ones_where(iota((256, 256), 0) < iota((256, 256), 1))
    before = dot(ones_where(member), earlier, ((1,), (0,)))
    second = jnp.sum(jnp.where(member, before, 0.0), axis=0, keepdims=True).astype(jnp.int32)
    place = (groups >> 5) * 128 + second * 32 + (groups & 31)
    n = iota((512, 256), 0)
    hot = ones_where((n & 447) == place)
    onehot[...] = hot
    loads[3].wait()
    loads[4].wait()
    moved = dot(jnp.concatenate([t_in[...], w_in[...]], axis=0), hot, ((1,), (1,)))
    moved = jnp.where((iota((32, 512), 1) & 64) == 0, moved[0:32], moved[32:64]).astype(BF16)
    for k in range(4):
        tx_g[k, 0:32, :] = moved[:, 128 * k : 128 * k + 128]

    for load in loads[5:]:
        load.wait()
    row, lane = iota((16, 128), 0), iota((16, 128), 1)
    tile = jnp.zeros((16, 128), F32)
    for j, ref in enumerate((op_in, tp_in, sw_in, tw_in)):
        v = ref[...]
        v = jnp.broadcast_to(jnp.concatenate([v, v], axis=1), (16, 128))
        for s, part in enumerate(split3(v)):
            tile = jnp.where(row == 3 * j + s, part.astype(F32), tile)
    tile = jnp.where((lane >> 6) == (a & 1), tile, 0.0)
    c_sum = jnp.sum(c_t.astype(F32), axis=0, keepdims=True)
    for k in range(2):
        v = jnp.broadcast_to(c_sum[:, 128 * k : 128 * k + 128], (16, 128))
        full = tile
        for s, part in enumerate(split3(v)):
            full = jnp.where(row == 12 + s, part.astype(F32), full)
        for half in range(2):
            tx_g[2 * k + half, 32:48, :] = full.astype(BF16)

    @pl.when(counts)
    def _():
        pl.semaphore_wait(line_sem, 1)

    @pl.when(jnp.logical_not(counts))
    def _():
        pl.semaphore_wait(bar, 7)

    @pl.when(jnp.logical_or(jnp.logical_and(core == 1, mine), jnp.logical_and(core == 0, (a ^ 1) == b_hi)))
    def _():
        tell(line_sem, [sibling])

    def c_copy(to):
        return pltpu.make_async_remote_copy(
            src_ref=tx_c.at[to],
            dst_ref=rx_c.at[a * 32 + b_lo],
            send_sem=c_send,
            recv_sem=c_recv,
            device_id=(to, b_hi),
            device_id_type=MESH,
        )

    def g_copy(k):
        to = (a + k) & 3
        return pltpu.make_async_remote_copy(
            src_ref=tx_g.at[to],
            dst_ref=rx_g.at[a],
            send_sem=g_send,
            recv_sem=g_recv,
            device_id=(b, to),
            device_id_type=MESH,
        )

    for k in range(1, 4):
        g_copy(k).start()

    @pl.when(jnp.logical_and(counts_early, b_hi < 2))
    def _():
        count_early()

    @pl.when(jnp.logical_not(counts_early))
    def _():
        pl.semaphore_wait(early_sem, 1)

    @pl.when(mine)
    def _():
        pltpu.make_async_copy(tx_c.at[b], rx_c.at[a * 32 + b_lo], c_recv).start()

    def early_step(j, carry):
        c_copy(j ^ 40 ^ (b & 63)).start()
        return carry

    lax.fori_loop(0, 40, early_step, 0, unroll=8)

    @pl.when(jnp.logical_not(jnp.logical_and(mine, b < 64)))
    def _():
        c_copy(b & 63).start()

    lax.fori_loop(41, 64, early_step, 0, unroll=23)

    def between(members):
        for j in members:
            to = (64 + j) ^ (b & 19)

            @pl.when(jnp.logical_not(jnp.logical_and(mine, b == to)))
            def _():
                c_copy(to).start()

    between([j for j in range(32) if j & 15 < 4])
    rx_g[a] = tx_g[a]

    def await_bytes(ref, sem):
        pltpu.make_async_copy(ref, ref, sem).wait()

    await_bytes(rx_g.at[pl.ds(0, 3)], g_recv)
    for k in range(4):
        both = rx_g[k, 0:32, :].astype(F32)
        other = pltpu.roll(both, 64, 1)
        in_first = iota((32, 128), 1) < 64
        t_s[32 * k : 32 * k + 32, :] = jnp.where(in_first, both, other)
        w_s[32 * k : 32 * k + 32, :] = jnp.where(in_first, other, both)
    parts = [rx_g[k, 32:48, :].astype(F32) for k in range(4)]
    parts = [parts[0] + parts[1], parts[2] + parts[3]]
    m, n = iota((32, 512), 0), iota((32, 512), 1)
    pick = jnp.logical_and(
        (m >> 4) == ((n & 127) >> 6),
        jnp.logical_and((m & 15) // 3 == (n >> 7), (m & 15) < 12),
    )
    spread = dot(
        jnp.transpose(jnp.concatenate(parts, axis=0)).astype(BF16), ones_where(pick), ((1,), (0,))
    )
    prm[0] = spread[:, 0:128] * (-1.66 * LOG2E)
    prm[1] = spread[:, 128:256] * LOG2E
    prm[2] = spread[:, 256:384]
    prm[3] = spread[:, 384:512]

    power = [prm[1, 8 * i : 8 * i + 8, :] for i in range(16)]

    def absorb(k, sums):
        sums = list(sums)
        rows_t = [jnp.broadcast_to(t_s[pl.ds(4 * k + u, 1), :], (8, 128)) for u in range(4)]
        rows_w = [jnp.broadcast_to(w_s[pl.ds(4 * k + u, 1), :], (8, 128)) for u in range(4)]
        for u in range(4):
            for i in range(16):
                x = rows_w[u] * jnp.exp2(power[i] * rows_t[u])
                xs[4 * k + u, 8 * i : 8 * i + 8, :] = x
                sums[i] = sums[i] + x
        return tuple(sums)

    sums = tuple(jnp.zeros((8, 128), F32) for i in range(16))
    for k in range(4):
        for i in range(16):
            above[k, 8 * i : 8 * i + 8, :] = sums[i]
        sums = lax.fori_loop(8 * k, 8 * k + 8, absorb, sums)

    sums = jnp.transpose(jnp.concatenate(sums, axis=0))
    for k in range(4):
        tx_s[:, k, :] = sums[32 * k : 32 * k + 32]

    @pl.when(mine)
    def _():
        pltpu.make_async_copy(tx_s.at[b_lo], rx_s.at[b_lo], s_recv).start()

    def s_send(to):
        pltpu.make_async_remote_copy(
            src_ref=tx_s.at[to],
            dst_ref=rx_s.at[b_lo],
            send_sem=s_send_sem,
            recv_sem=s_recv,
            device_id=(32 * a + to, b_hi),
            device_id_type=MESH,
        ).start()

    def s_sends(to_late):
        @pl.when(a == 2)
        def _():
            def step(to, carry):
                wanted = is_late(64 + to) == to_late

                @pl.when(jnp.logical_and(wanted, jnp.logical_not(jnp.logical_and(mine, to == b_lo))))
                def _():
                    s_send(to)

                return carry

            lax.fori_loop(0, 32, step, 0)

        @pl.when(a == 3 if to_late else a < 2)
        def _():
            @pl.when(jnp.logical_not(mine))
            def _():
                s_send(b_lo)

            def step(j, carry):
                s_send((b_lo + j) & 31)
                return carry

            lax.fori_loop(1, 32, step, 0, unroll=31)

    s_sends(False)

    @pl.when(counts_late)
    def _():
        pl.semaphore_wait(bar, LATE + 7)
        tell(late_sem, line)

    @pl.when(jnp.logical_not(counts_late))
    def _():
        pl.semaphore_wait(late_sem, 1)

    def late_step(j, carry):
        c_copy(96 + (j ^ 8 ^ b_lo)).start()
        return carry

    lax.fori_loop(0, 8, late_step, 0, unroll=8)

    @pl.when(jnp.logical_not(jnp.logical_and(mine, b >= 96)))
    def _():
        c_copy(96 + b_lo).start()

    lax.fori_loop(9, 32, late_step, 0, unroll=23)
    between([j for j in range(32) if j & 15 >= 4])

    s_sends(True)

    weight = [prm[3, 8 * i : 8 * i + 8, :] for i in range(16)]

    def radiate(k, carry):
        k = pl.multiple_of(8 * k, 8)
        for u in range(8):
            q = jnp.broadcast_to(1.0 + 0.2 * t_s[pl.ds(k + u, 1), :], (8, 128))
            for i in range(16):
                emit[k + u, 8 * i : 8 * i + 8, :] = weight[i] * q
        return carry

    lax.fori_loop(0, 16, radiate, 0)

    m, n = iota((256, 512), 0), iota((256, 512), 1)
    slot = m & 127
    pick = jnp.logical_and((slot >> 5) == (n >> 7), (n & 63) == (m >> 7) * 32 + (slot & 31))
    pick = ones_where(pick)
    await_bytes(rx_c, c_recv)
    got = jnp.transpose(rx_c[:, 0, :])
    both = jnp.concatenate([got[0:32], got[32:64]], axis=1).astype(BF16)
    cond = dot(both, pick, ((1,), (0,)))
    c_sums = jnp.zeros((1, 128), F32)
    for k in range(4):
        part = cond[:, 128 * k : 128 * k + 128]
        c_s[32 * k : 32 * k + 32, :] = part
        c_above[k] = jnp.broadcast_to(c_sums, (8, 128))
        c_sums = c_sums + jnp.sum(part, axis=0, keepdims=True)
    sun = got[64:72]
    first = sun[0:1] + sun[1:2] + sun[2:3]
    second = jnp.broadcast_to(sun[3:4] + sun[4:5] + sun[5:6], (8, 128))
    lane = iota((8, 128), 1)
    sun = jnp.where((lane & 63) < 32, jnp.broadcast_to(first, (8, 128)), pltpu.roll(second, 32, 1))
    sun = jnp.where(lane < 64, sun, 0.0)
    sun = sun + pltpu.roll(sun, 64, 1)

    def h_copy(to):
        return pltpu.make_async_remote_copy(
            src_ref=tx_h.at[to],
            dst_ref=rx_h.at[a],
            send_sem=h_send,
            recv_sem=h_recv,
            device_id=(b, to),
            device_id_type=MESH,
        )

    def levels(first, trans):
        rows_c = [jnp.broadcast_to(c_s[pl.ds(first + u, 1), :], (8, 128)) for u in range(UNROLL)]
        totals = [None] * UNROLL
        trans = list(trans)
        for u in range(UNROLL):
            for i in range(16):
                rows = slice(8 * i, 8 * i + 8)
                e = jnp.exp2(prm[0, rows, :] * (xs[first + u, rows, :] + rows_c[u]))
                term = (1.0 - e) * (trans[i] - emit[first + u, rows, :])
                trans[i] = trans[i] * e
                totals[u] = term if i == 0 else totals[u] + term
        for u in range(UNROLL):
            acc[first + u] = totals[u]
        return tuple(trans)

    def quarter(step, carry):
        def turn(*parts):
            part = parts[3]
            for k in range(3):
                part = jnp.where(step == k, parts[k], part)
            return part

        part = jnp.where(a == 0, turn(2, 1, 3, 0), jnp.where(a == 1, turn(0, 3, 2, 1), jnp.where(a == 2, turn(0, 1, 3, 2), step)))
        first = pl.multiple_of(32 * part, 32)
        c = c_above[part]
        trans = []
        for i in range(16):
            rows = slice(8 * i, 8 * i + 8)
            depth = prm[0, rows, :] * (above[part, rows, :] + c)
            trans.append(prm[2, rows, :] * sun * jnp.exp2(depth))
        lax.fori_loop(
            0, 32 // UNROLL, lambda k, v: levels(pl.multiple_of(first + UNROLL * k, UNROLL), v), tuple(trans)
        )
        heat = 0.0625 * jnp.sum(acc[pl.ds(first, 32)], axis=1)
        heat = heat + pltpu.roll(heat, 64, 1)

        @pl.when(step == 3)
        def _():
            rx_h[part] = heat

        @pl.when(step < 3)
        def _():
            tx_h[part] = heat
            h_copy(part).start()

        return carry

    lax.fori_loop(0, 4, quarter, 0)

    await_bytes(rx_s, s_recv)
    lane, row = iota((32, 128), 1), iota((32, 128), 0)
    c_all = jnp.broadcast_to(
        jnp.sum(parts[0][12:15] + parts[1][12:15], axis=0, keepdims=True), (32, 128)
    )
    mu_all = jnp.broadcast_to(mu_in[...], (32, 256))
    lane2, row2 = iota((32, 256), 1), iota((32, 256), 0)
    rows = None
    for r in range(2):
        at = 2 * row + r
        c_col = jnp.sum(jnp.where(lane == (a & 1) * 64 + at, c_all, 0.0), axis=1, keepdims=True)
        mu_col = jnp.sum(
            jnp.where(lane2 == a * 64 + 2 * row2 + r, mu_all, 0.0), axis=1, keepdims=True
        )
        flux = None
        for half in range(2):
            par = parts[half]
            factor = jnp.sum(par[0:3], axis=0, keepdims=True) * (-1.66 * LOG2E)
            weight = jnp.sum(par[6:9], axis=0, keepdims=True)
            term = weight * jnp.exp2(factor * (rx_s[:, 2 * half + r, :] + c_col))
            flux = term if flux is None else flux + term
        flux = jnp.sum(flux, axis=1, keepdims=True) * jnp.maximum(mu_col, 0.0)
        flux = jnp.where(lane == at, flux, 0.0)
        rows = flux if rows is None else rows + flux
    surf_ref[...] = jnp.sum(rows, axis=0, keepdims=True)[:, 0:64]

    await_bytes(rx_h.at[pl.ds(0, 3)], h_recv)
    heat = jnp.concatenate([rx_h[k] for k in range(4)], axis=1)
    heat = jnp.where((iota((32, 512), 1) & 127) < 64, heat, 0.0)
    heat = dot(jnp.concatenate(split3(heat), axis=0), onehot[...], ((1,), (0,)))
    heat_ref[...] = heat[0:32] + heat[32:64] + heat[64:96]

    await_bytes(tx_g.at[pl.ds(0, 3)], g_send)
    await_bytes(tx_h.at[pl.ds(0, 3)], h_send)

    @pl.when(mine)
    def _():
        await_bytes(tx_c.at[pl.ds(0, 127)], c_send)
        await_bytes(tx_s.at[pl.ds(0, 31)], s_send_sem)

    @pl.when(jnp.logical_not(mine))
    def _():
        await_bytes(tx_c, c_send)
        await_bytes(tx_s, s_send_sem)


def place(heat_in, surf_in, heat_out, surf_out, sem):
    copies = [
        pltpu.make_async_copy(heat_in, heat_out, sem.at[0]),
        pltpu.make_async_copy(surf_in, surf_out, sem.at[1]),
    ]
    for copy in copies:
        copy.start()
    for copy in copies:
        copy.wait()


def shards(
    thermal_deviation, moisture_mass, condensate_optic, sun_height_factor, group_assignment,
    opacity_factor, thermal_power, sunlight_weights, thermal_weights,
):
    vmem = pl.BlockSpec(memory_space=pltpu.VMEM)
    heating, surface = pl.pallas_call(
        kernel,
        out_shape=(
            jax.ShapeDtypeStruct((32, 256), F32),
            jax.ShapeDtypeStruct((1, 64), F32),
        ),
        in_specs=[pl.BlockSpec(memory_space=pltpu.HBM)] * 9,
        out_specs=(vmem, vmem),
        scratch_shapes=[
            pltpu.VMEM((32, 256), BF16),
            pltpu.VMEM((32, 256), BF16),
            pltpu.VMEM((32, 256), BF16),
            pltpu.VMEM((1, 256), F32),
            pltpu.VMEM((1, 256), jnp.int32),
            pltpu.VMEM((1, 64), F32),
            pltpu.VMEM((1, 64), F32),
            pltpu.VMEM((1, 64), F32),
            pltpu.VMEM((1, 64), F32),
            pltpu.VMEM((128, 1, 128), F32),
            pltpu.VMEM((128, 1, 128), F32),
            pltpu.VMEM((4, 48, 128), BF16),
            pltpu.VMEM((4, 48, 128), BF16),
            pltpu.VMEM((4, 32, 128), F32),
            pltpu.VMEM((4, 32, 128), F32),
            pltpu.VMEM((32, 4, 128), F32),
            pltpu.VMEM((32, 4, 128), F32),
            pltpu.VMEM((512, 256), BF16),
            pltpu.VMEM((128, 128), F32),
            pltpu.VMEM((128, 128), F32),
            pltpu.VMEM((128, 128), F32),
            pltpu.VMEM((4, 8, 128), F32),
            pltpu.VMEM((4, 128, 128), F32),
            pltpu.VMEM((128, 8, 128), F32),
            pltpu.VMEM((128, 128, 128), F32),
            pltpu.VMEM((128, 128, 128), F32),
            pltpu.VMEM((4, 128, 128), F32),
            pltpu.SemaphoreType.DMA((9,)),
        ]
        + [pltpu.SemaphoreType.DMA] * 8
        + [pltpu.SemaphoreType.REGULAR] * 3,
        compiler_params=pltpu.CompilerParams(
            collective_id=0, has_side_effects=True, vmem_limit_bytes=32 * 1024 * 1024
        ),
    )(
        *(
            pltpu.with_memory_space_constraint(v, pltpu.HBM)
            for v in (
                thermal_deviation.T,
                moisture_mass.T,
                condensate_optic.T,
                sun_height_factor.reshape(1, -1),
                group_assignment.reshape(1, -1),
                opacity_factor.reshape(1, -1),
                thermal_power.reshape(1, -1),
                sunlight_weights.reshape(1, -1),
                thermal_weights.reshape(1, -1),
            )
        )
    )
    heating, surface = pl.pallas_call(
        place,
        out_shape=(
            jax.ShapeDtypeStruct((32, 256), F32),
            jax.ShapeDtypeStruct((1, 64), F32),
        ),
        in_specs=[vmem] * 2,
        out_specs=[pl.BlockSpec(memory_space=pltpu.HBM)] * 2,
        scratch_shapes=[pltpu.SemaphoreType.DMA((2,))],
    )(*(pltpu.with_memory_space_constraint(v, pltpu.VMEM) for v in (heating, surface)))
    return heating.T, surface.reshape(-1)


def solution(mesh):
    in_specs = (
        P("blk", "ga"), P("blk", "ga"), P("blk", "ga"), P("blk"), P("blk"),
        P("ga"), P("ga"), P("ga"), P("ga"),
    )
    out_specs = (P("blk", "ga"), P(("blk", "ga")))
    return jax.shard_map(shards, mesh=mesh, in_specs=in_specs, out_specs=out_specs, check_vma=False)
```

```python
import jax
import jax.numpy as jnp
from jax import lax
from jax.experimental import pallas as pl
from jax.experimental.pallas import tpu as pltpu
from jax.sharding import PartitionSpec as P

F32 = jnp.float32
BF16 = jnp.bfloat16
UNROLL = 8
LOG2E = 1.4426950408889634
MESH = pl.DeviceIdType.MESH


def iota(shape, dim):
    return lax.broadcasted_iota(jnp.int32, shape, dim)


def split3(v):
    hi = v.astype(BF16)
    rest = v - hi.astype(F32)
    mid = rest.astype(BF16)
    lo = (rest - mid.astype(F32)).astype(BF16)
    return hi, mid, lo


def dot(x, y, dims):
    return lax.dot_general(x, y, (dims, ((), ())), preferred_element_type=F32)


def ones_where(cond):
    return jnp.where(cond, 1.0, 0.0).astype(BF16)


EARLY, LATE = 72, 56


def is_late(blk):
    return jnp.logical_or(blk >= 96, jnp.logical_and(blk >= 64, (blk & 15) >= 4))


def kernel(
    t_hbm, w_hbm, c_hbm, mu_hbm, g_hbm, op_hbm, tp_hbm, sw_hbm, tw_hbm,
    heat_ref, surf_ref,
    t_in, w_in, c_in, mu_in, g_in, op_in, tp_in, sw_in, tw_in,
    tx_c, rx_c, tx_g, rx_g, tx_h, rx_h, tx_s, rx_s,
    onehot, t_s, w_s, c_s, c_above, prm, acc, xs, emit, above,
    in_sem, c_send, c_recv, g_send, g_recv, h_send, h_recv, s_send_sem, s_recv, line_sem, early_sem, late_sem,
):
    b = lax.axis_index("blk")
    a = lax.axis_index("ga")
    b_hi, b_lo = b >> 5, b & 31
    mine = b_hi == a
    core = b & 1
    late = is_late(b)
    sibling = (b ^ 1, a)
    line = [(b, a ^ k) for k in range(1, 4)] + [(b ^ 1, a ^ k) for k in range(4)]
    counts_early = jnp.logical_and(core == 0, mine)
    counts_late = jnp.logical_and(core == 1, (a ^ 1) == b_hi)
    counts = jnp.logical_or(counts_early, counts_late)

    loads = [
        pltpu.make_async_copy(src, dst, in_sem.at[i])
        for i, (src, dst) in enumerate(
            (
                (c_hbm, c_in), (mu_hbm, mu_in), (g_hbm, g_in), (t_hbm, t_in), (w_hbm, w_in),
                (op_hbm, op_in), (tp_hbm, tp_in), (sw_hbm, sw_in), (tw_hbm, tw_in),
            )
        )
    ]
    for load in loads:
        load.start()

    bar = pltpu.get_barrier_semaphore()

    def greet(dev):
        pl.semaphore_signal(bar, inc=1, device_id=dev, device_id_type=MESH)

    for dev in line:
        greet(dev)
    self_counted = jnp.logical_and(counts_early, jnp.logical_not(late))
    told = jnp.where(late, a ^ 1, a)

    def announce(m):
        greet((32 * a + ((2 * m) ^ (b_lo & 30)) + jnp.where(late, 1, 0), told))

    for m in (4, 12, 5, 13, 3, 11, 6, 14, 2, 10, 7, 15, 1, 9, 8):
        announce(m)

    @pl.when(jnp.logical_not(self_counted))
    def _():
        announce(0)

    loads[0].wait()
    loads[1].wait()
    c_t = c_in[...]
    sun_row = jnp.maximum(mu_in[...], 0.0)
    row, col = iota((16, 512), 0), iota((16, 512), 1)
    sun_two = jnp.broadcast_to(jnp.concatenate([sun_row, sun_row], axis=1), (16, 512))
    sun_tile = jnp.zeros((16, 512), F32)
    for s, part in enumerate(split3(sun_two)):
        sun_tile = jnp.where(row == 3 * (col >> 8) + s, part.astype(F32), sun_tile)
    none = jnp.zeros((32, 256), BF16)
    laid = jnp.concatenate(
        [
            jnp.concatenate([c_t, none], axis=1),
            jnp.concatenate([none, c_t], axis=1),
            sun_tile.astype(BF16),
            jnp.zeros((48, 512), BF16),
        ],
        axis=0,
    )
    row, col = iota((128, 512), 0), iota((128, 512), 1)
    pick = ones_where((col & 255) == 2 * row + (col >> 8))
    tx_c[:, 0, :] = dot(pick, laid, ((1,), (1,)))

    def tell(sem, devices):
        for dev in devices:
            pl.semaphore_signal(sem, inc=1, device_id=dev, device_id_type=MESH)

    def count_early():
        pl.semaphore_wait(bar, EARLY + 7 - jnp.where(self_counted, 1, 0))
        tell(early_sem, line)

    @pl.when(jnp.logical_and(counts_early, b_hi >= 2))
    def _():
        count_early()

    loads[2].wait()
    groups = g_in[...]
    member = groups == iota((128, 256), 0)
    earlier = ones_where(iota((256, 256), 0) < iota((256, 256), 1))
    before = dot(ones_where(member), earlier, ((1,), (0,)))
    second = jnp.sum(jnp.where(member, before, 0.0), axis=0, keepdims=True).astype(jnp.int32)
    place = (groups >> 5) * 128 + second * 32 + (groups & 31)
    n = iota((512, 256), 0)
    hot = ones_where((n & 447) == place)
    onehot[...] = hot
    loads[3].wait()
    loads[4].wait()
    moved = dot(jnp.concatenate([t_in[...], w_in[...]], axis=0), hot, ((1,), (1,)))
    moved = jnp.where((iota((32, 512), 1) & 64) == 0, moved[0:32], moved[32:64]).astype(BF16)
    for k in range(4):
        tx_g[k, 0:32, :] = moved[:, 128 * k : 128 * k + 128]

    for load in loads[5:]:
        load.wait()
    row, lane = iota((16, 128), 0), iota((16, 128), 1)
    tile = jnp.zeros((16, 128), F32)
    for j, ref in enumerate((op_in, tp_in, sw_in, tw_in)):
        v = ref[...]
        v = jnp.broadcast_to(jnp.concatenate([v, v], axis=1), (16, 128))
        for s, part in enumerate(split3(v)):
            tile = jnp.where(row == 3 * j + s, part.astype(F32), tile)
    tile = jnp.where((lane >> 6) == (a & 1), tile, 0.0)
    c_sum = jnp.sum(c_t.astype(F32), axis=0, keepdims=True)
    for k in range(2):
        v = jnp.broadcast_to(c_sum[:, 128 * k : 128 * k + 128], (16, 128))
        full = tile
        for s, part in enumerate(split3(v)):
            full = jnp.where(row == 12 + s, part.astype(F32), full)
        for half in range(2):
            tx_g[2 * k + half, 32:48, :] = full.astype(BF16)

    @pl.when(counts)
    def _():
        pl.semaphore_wait(line_sem, 1)

    @pl.when(jnp.logical_not(counts))
    def _():
        pl.semaphore_wait(bar, 7)

    @pl.when(jnp.logical_or(jnp.logical_and(core == 1, mine), jnp.logical_and(core == 0, (a ^ 1) == b_hi)))
    def _():
        tell(line_sem, [sibling])

    def c_copy(to):
        return pltpu.make_async_remote_copy(
            src_ref=tx_c.at[to],
            dst_ref=rx_c.at[a * 32 + b_lo],
            send_sem=c_send,
            recv_sem=c_recv,
            device_id=(to, b_hi),
            device_id_type=MESH,
        )

    def g_copy(k):
        to = (a + k) & 3
        return pltpu.make_async_remote_copy(
            src_ref=tx_g.at[to],
            dst_ref=rx_g.at[a],
            send_sem=g_send,
            recv_sem=g_recv,
            device_id=(b, to),
            device_id_type=MESH,
        )

    for k in range(1, 4):
        g_copy(k).start()

    @pl.when(jnp.logical_and(counts_early, b_hi < 2))
    def _():
        count_early()

    @pl.when(jnp.logical_not(counts_early))
    def _():
        pl.semaphore_wait(early_sem, 1)

    @pl.when(mine)
    def _():
        pltpu.make_async_copy(tx_c.at[b], rx_c.at[a * 32 + b_lo], c_recv).start()

    def early_step(j, carry):
        c_copy(j ^ 40 ^ (b & 63)).start()
        return carry

    lax.fori_loop(0, 40, early_step, 0, unroll=8)

    @pl.when(jnp.logical_not(jnp.logical_and(mine, b < 64)))
    def _():
        c_copy(b & 63).start()

    lax.fori_loop(41, 64, early_step, 0, unroll=23)

    def between(members):
        for j in members:
            to = (64 + j) ^ (b & 19)

            @pl.when(jnp.logical_not(jnp.logical_and(mine, b == to)))
            def _():
                c_copy(to).start()

    between([j for j in range(32) if j & 15 < 4])
    rx_g[a] = tx_g[a]

    def await_bytes(ref, sem):
        pltpu.make_async_copy(ref, ref, sem).wait()

    await_bytes(rx_g.at[pl.ds(0, 3)], g_recv)
    for k in range(4):
        both = rx_g[k, 0:32, :].astype(F32)
        other = pltpu.roll(both, 64, 1)
        in_first = iota((32, 128), 1) < 64
        t_s[32 * k : 32 * k + 32, :] = jnp.where(in_first, both, other)
        w_s[32 * k : 32 * k + 32, :] = jnp.where(in_first, other, both)
    parts = [rx_g[k, 32:48, :].astype(F32) for k in range(4)]
    parts = [parts[0] + parts[1], parts[2] + parts[3]]
    m, n = iota((32, 512), 0), iota((32, 512), 1)
    pick = jnp.logical_and(
        (m >> 4) == ((n & 127) >> 6),
        jnp.logical_and((m & 15) // 3 == (n >> 7), (m & 15) < 12),
    )
    spread = dot(
        jnp.transpose(jnp.concatenate(parts, axis=0)).astype(BF16), ones_where(pick), ((1,), (0,))
    )
    prm[0] = spread[:, 0:128] * (-1.66 * LOG2E)
    prm[1] = spread[:, 128:256] * LOG2E
    prm[2] = spread[:, 256:384]
    prm[3] = spread[:, 384:512]

    power = [prm[1, 8 * i : 8 * i + 8, :] for i in range(16)]

    def absorb(k, sums):
        sums = list(sums)
        rows_t = [jnp.broadcast_to(t_s[pl.ds(4 * k + u, 1), :], (8, 128)) for u in range(4)]
        rows_w = [jnp.broadcast_to(w_s[pl.ds(4 * k + u, 1), :], (8, 128)) for u in range(4)]
        for u in range(4):
            for i in range(16):
                x = rows_w[u] * jnp.exp2(power[i] * rows_t[u])
                xs[4 * k + u, 8 * i : 8 * i + 8, :] = x
                sums[i] = sums[i] + x
        return tuple(sums)

    sums = tuple(jnp.zeros((8, 128), F32) for i in range(16))
    for k in range(4):
        for i in range(16):
            above[k, 8 * i : 8 * i + 8, :] = sums[i]
        sums = lax.fori_loop(8 * k, 8 * k + 8, absorb, sums)

    sums = jnp.transpose(jnp.concatenate(sums, axis=0))
    for k in range(4):
        tx_s[:, k, :] = sums[32 * k : 32 * k + 32]

    @pl.when(mine)
    def _():
        pltpu.make_async_copy(tx_s.at[b_lo], rx_s.at[b_lo], s_recv).start()

    def s_send(to):
        pltpu.make_async_remote_copy(
            src_ref=tx_s.at[to],
            dst_ref=rx_s.at[b_lo],
            send_sem=s_send_sem,
            recv_sem=s_recv,
            device_id=(32 * a + to, b_hi),
            device_id_type=MESH,
        ).start()

    def s_sends(to_late):
        @pl.when(a == 2)
        def _():
            def step(to, carry):
                wanted = is_late(64 + to) == to_late

                @pl.when(jnp.logical_and(wanted, jnp.logical_not(jnp.logical_and(mine, to == b_lo))))
                def _():
                    s_send(to)

                return carry

            lax.fori_loop(0, 32, step, 0)

        @pl.when(a == 3 if to_late else a < 2)
        def _():
            @pl.when(jnp.logical_not(mine))
            def _():
                s_send(b_lo)

            def step(j, carry):
                s_send((b_lo + j) & 31)
                return carry

            lax.fori_loop(1, 32, step, 0, unroll=31)

    s_sends(False)

    @pl.when(counts_late)
    def _():
        pl.semaphore_wait(bar, LATE + 7)
        tell(late_sem, line)

    @pl.when(jnp.logical_not(counts_late))
    def _():
        pl.semaphore_wait(late_sem, 1)

    def late_step(j, carry):
        c_copy(96 + (j ^ 8 ^ b_lo)).start()
        return carry

    lax.fori_loop(0, 8, late_step, 0, unroll=8)

    @pl.when(jnp.logical_not(jnp.logical_and(mine, b >= 96)))
    def _():
        c_copy(96 + b_lo).start()

    lax.fori_loop(9, 32, late_step, 0, unroll=23)
    between([j for j in range(32) if j & 15 >= 4])

    s_sends(True)

    weight = [prm[3, 8 * i : 8 * i + 8, :] for i in range(16)]

    def radiate(k, carry):
        k = pl.multiple_of(8 * k, 8)
        for u in range(8):
            q = jnp.broadcast_to(1.0 + 0.2 * t_s[pl.ds(k + u, 1), :], (8, 128))
            for i in range(16):
                emit[k + u, 8 * i : 8 * i + 8, :] = weight[i] * q
        return carry

    lax.fori_loop(0, 16, radiate, 0)

    m, n = iota((256, 512), 0), iota((256, 512), 1)
    slot = m & 127
    pick = jnp.logical_and((slot >> 5) == (n >> 7), (n & 63) == (m >> 7) * 32 + (slot & 31))
    pick = ones_where(pick)
    await_bytes(rx_c, c_recv)
    got = jnp.transpose(rx_c[:, 0, :])
    both = jnp.concatenate([got[0:32], got[32:64]], axis=1).astype(BF16)
    cond = dot(both, pick, ((1,), (0,)))
    c_sums = jnp.zeros((1, 128), F32)
    for k in range(4):
        part = cond[:, 128 * k : 128 * k + 128]
        c_s[32 * k : 32 * k + 32, :] = part
        c_above[k] = jnp.broadcast_to(c_sums, (8, 128))
        c_sums = c_sums + jnp.sum(part, axis=0, keepdims=True)
    sun = got[64:72]
    first = sun[0:1] + sun[1:2] + sun[2:3]
    second = jnp.broadcast_to(sun[3:4] + sun[4:5] + sun[5:6], (8, 128))
    lane = iota((8, 128), 1)
    sun = jnp.where((lane & 63) < 32, jnp.broadcast_to(first, (8, 128)), pltpu.roll(second, 32, 1))
    sun = jnp.where(lane < 64, sun, 0.0)
    sun = sun + pltpu.roll(sun, 64, 1)

    def h_copy(to):
        return pltpu.make_async_remote_copy(
            src_ref=tx_h.at[to],
            dst_ref=rx_h.at[a],
            send_sem=h_send,
            recv_sem=h_recv,
            device_id=(b, to),
            device_id_type=MESH,
        )

    def levels(first, trans):
        rows_c = [jnp.broadcast_to(c_s[pl.ds(first + u, 1), :], (8, 128)) for u in range(UNROLL)]
        totals = [None] * UNROLL
        trans = list(trans)
        for u in range(UNROLL):
            for i in range(16):
                rows = slice(8 * i, 8 * i + 8)
                e = jnp.exp2(prm[0, rows, :] * (xs[first + u, rows, :] + rows_c[u]))
                term = (1.0 - e) * (trans[i] - emit[first + u, rows, :])
                trans[i] = trans[i] * e
                totals[u] = term if i == 0 else totals[u] + term
        for u in range(UNROLL):
            acc[first + u] = totals[u]
        return tuple(trans)

    def quarter(step, carry):
        def turn(*parts):
            part = parts[3]
            for k in range(3):
                part = jnp.where(step == k, parts[k], part)
            return part

        part = jnp.where(a == 0, turn(2, 1, 3, 0), jnp.where(a == 1, turn(0, 3, 2, 1), jnp.where(a == 2, turn(0, 1, 3, 2), step)))
        first = pl.multiple_of(32 * part, 32)
        c = c_above[part]
        trans = []
        for i in range(16):
            rows = slice(8 * i, 8 * i + 8)
            depth = prm[0, rows, :] * (above[part, rows, :] + c)
            trans.append(prm[2, rows, :] * sun * jnp.exp2(depth))
        lax.fori_loop(
            0, 32 // UNROLL, lambda k, v: levels(pl.multiple_of(first + UNROLL * k, UNROLL), v), tuple(trans)
        )
        heat = 0.0625 * jnp.sum(acc[pl.ds(first, 32)], axis=1)
        heat = heat + pltpu.roll(heat, 64, 1)
        heat = jnp.where(iota((16, 128), 1) < 64, heat[0:16], heat[16:32])

        @pl.when(step == 3)
        def _():
            rx_h[part] = heat

        @pl.when(step < 3)
        def _():
            tx_h[part] = heat
            h_copy(part).start()

        return carry

    lax.fori_loop(0, 4, quarter, 0)

    await_bytes(rx_s, s_recv)
    lane, row = iota((32, 128), 1), iota((32, 128), 0)
    c_all = jnp.broadcast_to(
        jnp.sum(parts[0][12:15] + parts[1][12:15], axis=0, keepdims=True), (32, 128)
    )
    mu_all = jnp.broadcast_to(mu_in[...], (32, 256))
    lane2, row2 = iota((32, 256), 1), iota((32, 256), 0)
    rows = None
    for r in range(2):
        at = 2 * row + r
        c_col = jnp.sum(jnp.where(lane == (a & 1) * 64 + at, c_all, 0.0), axis=1, keepdims=True)
        mu_col = jnp.sum(
            jnp.where(lane2 == a * 64 + 2 * row2 + r, mu_all, 0.0), axis=1, keepdims=True
        )
        flux = None
        for half in range(2):
            par = parts[half]
            factor = jnp.sum(par[0:3], axis=0, keepdims=True) * (-1.66 * LOG2E)
            weight = jnp.sum(par[6:9], axis=0, keepdims=True)
            term = weight * jnp.exp2(factor * (rx_s[:, 2 * half + r, :] + c_col))
            flux = term if flux is None else flux + term
        flux = jnp.sum(flux, axis=1, keepdims=True) * jnp.maximum(mu_col, 0.0)
        flux = jnp.where(lane == at, flux, 0.0)
        rows = flux if rows is None else rows + flux
    surf_ref[...] = jnp.sum(rows, axis=0, keepdims=True)[:, 0:64]

    await_bytes(rx_h.at[pl.ds(0, 3)], h_recv)
    heat = jnp.concatenate([rx_h[k] for k in range(4)], axis=1)
    in_first = (iota((16, 512), 1) & 64) == 0
    heat = jnp.concatenate([jnp.where(in_first, heat, 0.0), jnp.where(in_first, 0.0, heat)], axis=0)
    heat = dot(jnp.concatenate(split3(heat), axis=0), onehot[...], ((1,), (0,)))
    heat_ref[...] = heat[0:32] + heat[32:64] + heat[64:96]

    await_bytes(tx_g.at[pl.ds(0, 3)], g_send)
    await_bytes(tx_h.at[pl.ds(0, 3)], h_send)

    @pl.when(mine)
    def _():
        await_bytes(tx_c.at[pl.ds(0, 127)], c_send)
        await_bytes(tx_s.at[pl.ds(0, 31)], s_send_sem)

    @pl.when(jnp.logical_not(mine))
    def _():
        await_bytes(tx_c, c_send)
        await_bytes(tx_s, s_send_sem)


def place(heat_in, surf_in, heat_out, surf_out, sem):
    copies = [
        pltpu.make_async_copy(heat_in, heat_out, sem.at[0]),
        pltpu.make_async_copy(surf_in, surf_out, sem.at[1]),
    ]
    for copy in copies:
        copy.start()
    for copy in copies:
        copy.wait()


def shards(
    thermal_deviation, moisture_mass, condensate_optic, sun_height_factor, group_assignment,
    opacity_factor, thermal_power, sunlight_weights, thermal_weights,
):
    vmem = pl.BlockSpec(memory_space=pltpu.VMEM)
    heating, surface = pl.pallas_call(
        kernel,
        out_shape=(
            jax.ShapeDtypeStruct((32, 256), F32),
            jax.ShapeDtypeStruct((1, 64), F32),
        ),
        in_specs=[pl.BlockSpec(memory_space=pltpu.HBM)] * 9,
        out_specs=(vmem, vmem),
        scratch_shapes=[
            pltpu.VMEM((32, 256), BF16),
            pltpu.VMEM((32, 256), BF16),
            pltpu.VMEM((32, 256), BF16),
            pltpu.VMEM((1, 256), F32),
            pltpu.VMEM((1, 256), jnp.int32),
            pltpu.VMEM((1, 64), F32),
            pltpu.VMEM((1, 64), F32),
            pltpu.VMEM((1, 64), F32),
            pltpu.VMEM((1, 64), F32),
            pltpu.VMEM((128, 1, 128), F32),
            pltpu.VMEM((128, 1, 128), F32),
            pltpu.VMEM((4, 48, 128), BF16),
            pltpu.VMEM((4, 48, 128), BF16),
            pltpu.VMEM((4, 16, 128), F32),
            pltpu.VMEM((4, 16, 128), F32),
            pltpu.VMEM((32, 4, 128), F32),
            pltpu.VMEM((32, 4, 128), F32),
            pltpu.VMEM((512, 256), BF16),
            pltpu.VMEM((128, 128), F32),
            pltpu.VMEM((128, 128), F32),
            pltpu.VMEM((128, 128), F32),
            pltpu.VMEM((4, 8, 128), F32),
            pltpu.VMEM((4, 128, 128), F32),
            pltpu.VMEM((128, 8, 128), F32),
            pltpu.VMEM((128, 128, 128), F32),
            pltpu.VMEM((128, 128, 128), F32),
            pltpu.VMEM((4, 128, 128), F32),
            pltpu.SemaphoreType.DMA((9,)),
        ]
        + [pltpu.SemaphoreType.DMA] * 8
        + [pltpu.SemaphoreType.REGULAR] * 3,
        compiler_params=pltpu.CompilerParams(
            collective_id=0, has_side_effects=True, vmem_limit_bytes=32 * 1024 * 1024
        ),
    )(
        *(
            pltpu.with_memory_space_constraint(v, pltpu.HBM)
            for v in (
                thermal_deviation.T,
                moisture_mass.T,
                condensate_optic.T,
                sun_height_factor.reshape(1, -1),
                group_assignment.reshape(1, -1),
                opacity_factor.reshape(1, -1),
                thermal_power.reshape(1, -1),
                sunlight_weights.reshape(1, -1),
                thermal_weights.reshape(1, -1),
            )
        )
    )
    heating, surface = pl.pallas_call(
        place,
        out_shape=(
            jax.ShapeDtypeStruct((32, 256), F32),
            jax.ShapeDtypeStruct((1, 64), F32),
        ),
        in_specs=[vmem] * 2,
        out_specs=[pl.BlockSpec(memory_space=pltpu.HBM)] * 2,
        scratch_shapes=[pltpu.SemaphoreType.DMA((2,))],
    )(*(pltpu.with_memory_space_constraint(v, pltpu.VMEM) for v in (heating, surface)))
    return heating.T, surface.reshape(-1)


def solution(mesh):
    in_specs = (
        P("blk", "ga"), P("blk", "ga"), P("blk", "ga"), P("blk"), P("blk"),
        P("ga"), P("ga"), P("ga"), P("ga"),
    )
    out_specs = (P("blk", "ga"), P(("blk", "ga")))
    return jax.shard_map(shards, mesh=mesh, in_specs=in_specs, out_specs=out_specs, check_vma=False)
```
